32 devices in a mesh: groups: 2 (over y), serial: 4 (over z), level: 2 (over x), feat: 2 (over core).
Axes of the slice: x: 2, y: 2, z: 4, core: 2. Of those that a mesh axis runs over, the one named last changes fastest.
Arguments:
- points: bfloat16 [65536, 64], P(('groups', 'serial', 'level')), parts along dimension 0, may hold values from -6 to 6
- patch_ids: int32 [65536], P(('groups', 'serial', 'level')), parts along dimension 0, may hold values from 0 to 63, never falling along the last dimension, each value on 1 to 1024 neighbouring positions
- child_counts: int32 [16, 2048], P(('groups', 'serial', 'level')), parts along dimension 0, may hold values from 1 to 8, 4096 in all within a row
- voxel_slot: int32 [32768], P(('groups', 'serial', 'level')), parts along dimension 0, may hold values from 0 to 16383, as said below
- w_query0: bfloat16 [64, 64], P(None, 'feat'), may hold values from -2 to 2
- w_key0: bfloat16 [64, 64], P(None, 'feat'), may hold values from -2 to 2
- w_value0: bfloat16 [64, 64], P(None, 'feat'), may hold values from -6 to 6
- w_attn_out0: bfloat16 [64, 64], P('feat'), may hold values from -3 to 3
- w_mlp_in: bfloat16 [64, 256], P(None, 'feat'), may hold values from -0.75 to 0.75
- w_mlp_out: bfloat16 [256, 64], P('feat'), may hold values from -0.375 to 0.375
- w_pool: bfloat16 [64, 128], replicated, may hold values from -0.75 to 0.75
- w_query1: bfloat16 [128, 128], P(None, 'feat'), may hold values from -2 to 2
- w_key1: bfloat16 [128, 128], P(None, 'feat'), may hold values from -2 to 2
- w_value1: bfloat16 [128, 128], P(None, 'feat'), may hold values from -0.5 to 0.5
- w_attn_out1: bfloat16 [128, 128], P('feat'), may hold values from -0.5 to 0.5
- w_up: bfloat16 [128, 64], replicated, may hold values from -0.5 to 0.5
Outputs:
- refined: bfloat16 [65536, 64], P(('groups', 'serial', 'level')), parts along dimension 0
The draws below stay inside these ranges and needn't reach their ends.
There are 2 independent parts, one for each index of `groups`. The reference program is written for one: setup_inputs(seed, part) draws one part's arguments, and reference() takes and returns one part's arrays. A program takes and returns all parts, laid end to end along the dimension named above; an argument that names none is the same for every part. Nothing has to cross between parts.
Inputs may be any that keep to these rules, and one draw needn't show every extreme that they name: `patch_ids`: never falls along the points; each patch is a run of consecutive points. `child_counts`: each row sums to 4096. `voxel_slot`: A permutation of 0 to 16383. Position g belongs to shard g // 2048 (shard s * 2 + l has serial index s and level index l); a voxel goes to a shard of the same level index as its own shard; from one shard to one shard go at most 1024 voxels, and that many in some pair of every level index.
All inputs are finite; a program needn't handle non-finite values.
Results may differ from the reference program's by a relative error of at most 0.005.
The reference program's roundings to bfloat16 on the way count: a program that leaves them out, or rounds other values in their place, can miss the bound.
Values may be sent and summed in bfloat16 or wider, within the bound.
A program may use at most 64 MiB of HBM per device.

```python
import math
import jax
import jax.numpy as jnp
import numpy as np
from jax import lax

C0 = 64
C1 = 128
HEAD = 16
HID0 = 256
PATCH = 1024
Q_DEV = 2048
PTS_DEV = 4096
SHARDS = 8
POINTS = 32768
CAP = 1024
N_SERIAL = 4
N_LEVEL = 2


def level_slots(key, level_index):
    shard_count = N_SERIAL
    capacity = CAP
    per_shard = Q_DEV
    key_wiggle, key_roll, key_send, key_land = jax.random.split(key, 4)
    leftover_total = per_shard - capacity
    even_load = leftover_total // (shard_count - 1)
    leftover = leftover_total % (shard_count - 1)
    swing = even_load // 2
    lanes = jnp.arange(shard_count, dtype=jnp.int32)
    extra_one = ((lanes >= 1) & (lanes - 1 < leftover)).astype(jnp.int32)
    load_list = jnp.where(lanes == 0, capacity, even_load + extra_one).astype(jnp.int32)
    pair_count = (shard_count - 1) // 2
    if pair_count > 0 and swing > 0:
        wiggle = jax.random.randint(key_wiggle, (pair_count,), -swing, swing + 1)
        pair_lanes = jnp.arange(pair_count, dtype=jnp.int32)
        load_list = load_list.at[1 + 2 * pair_lanes].add(wiggle)
        load_list = load_list.at[2 + 2 * pair_lanes].add(-wiggle)
    load_list = jnp.roll(load_list, jax.random.randint(key_roll, (), 0, shard_count))
    run_of = jnp.repeat(lanes, load_list, total_repeat_length=per_shard)
    run_start = (jnp.cumsum(load_list) - load_list).astype(jnp.int32)
    run_rank = jnp.arange(per_shard, dtype=jnp.int32) - run_start[run_of]
    send_keys = jax.random.split(key_send, shard_count)
    orders = jax.vmap(lambda one_key: jax.random.permutation(one_key, per_shard))(send_keys)
    target = (lanes[:, None] + run_of[None, :]) % shard_count
    table = load_list[(lanes[:, None] - lanes[None, :]) % shard_count]
    offsets = (jnp.cumsum(table, axis=1) - table).astype(jnp.int32)
    arrival = offsets[target, lanes[:, None]] + run_rank[None, :]
    land_keys = jax.random.split(key_land, shard_count)
    landing = jax.vmap(lambda one_key: jax.random.permutation(one_key, per_shard))(land_keys)
    landed_row = landing[target, arrival]
    position = (target * N_LEVEL + level_index) * per_shard + landed_row
    result = jnp.zeros((shard_count, per_shard), jnp.int32)
    result = result.at[lanes[:, None], orders].set(position.astype(jnp.int32))
    return result


def draw_voxel_slot(key, part):
    key = jax.random.fold_in(key, 7)
    pieces = [level_slots(jax.random.fold_in(key, level_index), level_index) for level_index in range(N_LEVEL)]
    stacked = jnp.stack(pieces, axis=1)
    return stacked.reshape(-1).astype(jnp.int32)


def aligned_weight(shared, own_key, salt, fan_in, width, strengths, tilt):
    base = jax.random.fold_in(shared, salt)
    head_count = width // HEAD
    head_rank = jax.random.permutation(jax.random.fold_in(base, 1), head_count)
    table = jnp.zeros((head_count,), jnp.float32)
    for place in range(len(strengths)):
        table = jnp.where(head_rank == place, strengths[place], table)
    chosen_head = head_rank < len(strengths)
    column_strength = jnp.repeat(table, HEAD)
    chosen_column = jnp.repeat(chosen_head, HEAD)
    common = jax.random.uniform(jax.random.fold_in(base, 2), (fan_in, width), jnp.float32, -1.0, 1.0)
    common = common * jnp.sqrt(3.0 * column_strength)[None, :]
    own = jax.random.truncated_normal(jax.random.fold_in(own_key, 1), -3.0, 3.0, (fan_in, width), jnp.float32) * fan_in ** (-0.5)
    stretch = 1.0 + tilt * jax.random.uniform(jax.random.fold_in(own_key, 2), (fan_in, width), jnp.float32, -1.0, 1.0)
    result = jnp.where(chosen_column[None, :], common * stretch, own)
    return result.astype(jnp.bfloat16)


def draw_w_query0(key, part):
    shared = key
    key = jax.random.fold_in(key, 31)
    strengths = (0.02, 0.02)
    return aligned_weight(shared, key, 101, C0, C0, strengths, 0.0)


def draw_w_key0(key, part):
    shared = key
    key = jax.random.fold_in(key, 32)
    strengths = (0.02, 0.02)
    return aligned_weight(shared, key, 101, C0, C0, strengths, 0.1)


def draw_w_query1(key, part):
    shared = key
    key = jax.random.fold_in(key, 33)
    strengths = (0.01, 0.01, 0.01)
    return aligned_weight(shared, key, 102, C1, C1, strengths, 0.0)


def draw_w_key1(key, part):
    shared = key
    key = jax.random.fold_in(key, 34)
    strengths = (0.01, 0.01, 0.01)
    return aligned_weight(shared, key, 102, C1, C1, strengths, 0.1)


def block_levels(key, extent, cuts, low, top_value):
    factor_of, own = 1.0, jax.random.fold_in(key, 6)
    for dim, blocks in cuts:
        steps = jnp.exp(jax.random.uniform(jax.random.fold_in(own, dim), (blocks,), jnp.float32, low / len(cuts), top_value / len(cuts)))
        factor_of = factor_of * jnp.repeat(steps, extent[dim] // blocks).reshape([-1 if axis == dim else 1 for axis in range(len(extent))])
    return factor_of


def profile(count, total, most, skew):
    portions = [(1 << 20) // math.isqrt(rank ** skew) + 1 for rank in range(2, count + 1)]
    surplus, given = total - most - (count - 1), [1] * (count - 1)
    while surplus > 0:
        movable = [i for i in range(count - 1) if given[i] < most]
        mass, budget = sum([portions[i] for i in movable]), surplus
        for i in movable:
            extra = min(most - given[i], max(1, budget * portions[i] // mass), surplus)
            given[i] = given[i] + extra
            surplus = surplus - extra
    return np.array([most] + given)


def uneven_parts(key, number_of, total, limit, lean):
    if number_of == 2:
        one = jax.random.randint(key, (), max(1, total - limit), min(limit, total - 1) + 1)
        return jnp.stack([one, total - one])
    sizes = jnp.asarray(profile(number_of, total, limit, lean), jnp.int32)
    twos = (number_of - 1) // 2
    donor, sink = sizes[1:1 + 2 * twos:2], sizes[2:2 + 2 * twos:2]
    room = jnp.minimum(donor - 1, limit - sink)
    moved = jax.random.randint(jax.random.fold_in(key, 1), (twos,), 0, 1 << 20) % (room + 1)
    sizes = sizes.at[1:1 + 2 * twos:2].set(donor - moved).at[2:2 + 2 * twos:2].set(sink + moved)
    return sizes[jax.random.permutation(jax.random.fold_in(key, 2), number_of)]


def normal_values(rng, dims, scale, reach, cuts=(), held_as=jnp.bfloat16):
    factor_of = block_levels(rng, dims, cuts, -0.22, 0.18) if cuts else 1.0
    values = jax.random.normal(rng, dims, jnp.float32) * scale * factor_of
    return jnp.minimum(jnp.maximum(values, -reach), reach).astype(held_as)


def setup_inputs(seed: int = 0, part: int = 0) -> dict:
    streams_of = jax.random.split(jax.random.key(seed), 17)
    part_keys = jax.random.split(jax.random.fold_in(streams_of[16], part), 17)
    points = normal_values(part_keys[0], (POINTS, C0), 1.0, 6.0, ((0, 8),))
    patch_ids = jnp.searchsorted(jnp.cumsum(uneven_parts(part_keys[1], POINTS // (PATCH // 2), POINTS, PATCH, 1)), jnp.arange(POINTS), side="right").astype(jnp.int32)
    child_counts = jax.vmap(lambda own: uneven_parts(own, Q_DEV, PTS_DEV, 8, 1))(jax.random.split(part_keys[2], SHARDS)).reshape((SHARDS, Q_DEV)).astype(jnp.int32)
    voxel_slot = draw_voxel_slot(jax.random.fold_in(jax.random.fold_in(streams_of[16], part), 71), part)
    w_query0 = draw_w_query0(jax.random.fold_in(streams_of[16], 71), part)
    w_key0 = draw_w_key0(jax.random.fold_in(streams_of[16], 71), part)
    w_value0 = normal_values(streams_of[6], (C0, C0), 1 ** -0.5, 6.0, ((1, 2),))
    w_attn_out0 = normal_values(streams_of[7], (C0, C0), (C0 // 16) ** -0.5, 3.0, ((0, 2),))
    w_mlp_in = normal_values(streams_of[8], (C0, HID0), C0 ** -0.5, 0.75, ((1, 2),))
    w_mlp_out = normal_values(streams_of[9], (HID0, C0), HID0 ** -0.5, 0.375, ((0, 2),))
    w_pool = normal_values(streams_of[10], (C0, C1), C0 ** -0.5, 0.75)
    w_query1 = draw_w_query1(jax.random.fold_in(streams_of[16], 71), part)
    w_key1 = draw_w_key1(jax.random.fold_in(streams_of[16], 71), part)
    w_value1 = normal_values(streams_of[13], (C1, C1), C1 ** -0.5, 0.5, ((1, 2),))
    w_attn_out1 = normal_values(streams_of[14], (C1, C1), C1 ** -0.5, 0.5, ((0, 2),))
    w_up = normal_values(streams_of[15], (C1, C0), C1 ** -0.5, 0.5)
    return dict(points=points, patch_ids=patch_ids, child_counts=child_counts, voxel_slot=voxel_slot, w_query0=w_query0, w_key0=w_key0, w_value0=w_value0, w_attn_out0=w_attn_out0, w_mlp_in=w_mlp_in, w_mlp_out=w_mlp_out, w_pool=w_pool, w_query1=w_query1, w_key1=w_key1, w_value1=w_value1, w_attn_out1=w_attn_out1, w_up=w_up)


EPSILON = 1e-05
NEG_LARGE = -1e+30

def layer_norm(values):
    values = values.astype(jnp.float32)
    centre = values - lax.optimization_barrier(jnp.mean(values, axis=-1, keepdims=True))
    spread = lax.optimization_barrier(jnp.mean(centre * centre, axis=-1, keepdims=True))
    return centre * lax.rsqrt(spread + EPSILON)

def attend(queries, key_rows, value_rows, query_marks, key_marks):
    q_count = queries.shape[0]
    k_count = key_rows.shape[0]
    head_count = queries.shape[1] // HEAD
    q_heads = queries.astype(jnp.float32).reshape(q_count, head_count, HEAD)
    k_heads = key_rows.astype(jnp.float32).reshape(k_count, head_count, HEAD)
    v_heads = value_rows.astype(jnp.float32).reshape(k_count, head_count, HEAD)
    scores = jnp.einsum('qhd,khd->hqk', q_heads, k_heads) * HEAD ** (-0.5)
    allowed = (query_marks[:, None] == key_marks[None, :])[None, :, :]
    masked = jnp.where(allowed, scores, NEG_LARGE)
    topmost = lax.optimization_barrier(jnp.max(masked, axis=-1, keepdims=True))
    expweight = jnp.exp(masked - topmost)
    denominator = lax.optimization_barrier(jnp.sum(expweight, axis=-1))
    rounded = expweight.astype(jnp.bfloat16)
    mixed = jnp.einsum('hqk,khd->qhd', rounded.astype(jnp.float32), v_heads)
    mixed = mixed / jnp.transpose(denominator)[:, :, None]
    return mixed.reshape(q_count, head_count * HEAD).astype(jnp.bfloat16)

def project(values, weights):
    return jnp.dot(values, weights, preferred_element_type=jnp.float32)

def reference(points, patch_ids, child_counts, voxel_slot, w_query0, w_key0, w_value0, w_attn_out0, w_mlp_in, w_mlp_out, w_pool, w_query1, w_key1, w_value1, w_attn_out1, w_up):
    total_points = points.shape[0]
    normed0 = layer_norm(points).astype(jnp.bfloat16)
    query0 = project(normed0, w_query0).astype(jnp.bfloat16)
    key0 = project(normed0, w_key0).astype(jnp.bfloat16)
    value0 = project(normed0, w_value0).astype(jnp.bfloat16)
    padding = jnp.zeros((PATCH, C0), jnp.bfloat16)
    key_padded = jnp.concatenate([padding, key0, padding], axis=0)
    value_padded = jnp.concatenate([padding, value0, padding], axis=0)
    outside = jnp.full((PATCH,), -1, jnp.int32)
    patch_marks = patch_ids.astype(jnp.int32)
    marks_padded = jnp.concatenate([outside, patch_marks, outside], axis=0)

    def level_zero_block(block_index):
        start_row = (block_index * PATCH).astype(jnp.int32)
        queries = lax.dynamic_slice_in_dim(query0, start_row, PATCH, 0)
        key_rows = lax.dynamic_slice_in_dim(key_padded, start_row, 3 * PATCH, 0)
        value_rows = lax.dynamic_slice_in_dim(value_padded, start_row, 3 * PATCH, 0)
        query_marks = lax.dynamic_slice_in_dim(patch_marks, start_row, PATCH, 0)
        key_marks = lax.dynamic_slice_in_dim(marks_padded, start_row, 3 * PATCH, 0)
        return attend(queries, key_rows, value_rows, query_marks, key_marks)
    mixed0 = lax.map(level_zero_block, jnp.arange(total_points // PATCH, dtype=jnp.int32))
    mixed0 = mixed0.reshape(total_points, C0)
    hidden0 = (points.astype(jnp.float32) + project(mixed0, w_attn_out0)).astype(jnp.bfloat16)
    normed1 = layer_norm(hidden0).astype(jnp.bfloat16)
    inner = jax.nn.gelu(project(normed1, w_mlp_in)).astype(jnp.bfloat16)
    fine = (hidden0.astype(jnp.float32) + project(inner, w_mlp_out)).astype(jnp.bfloat16)
    counts_flat = child_counts.reshape(-1).astype(jnp.int32)
    voxel_total = counts_flat.shape[0]
    starts = (jnp.cumsum(counts_flat) - counts_flat).astype(jnp.int32)
    starts_marked = jnp.zeros((total_points,), jnp.int32).at[starts].add(1)
    parent = (jnp.cumsum(starts_marked) - 1).astype(jnp.int32)
    summed = jax.ops.segment_sum(fine.astype(jnp.float32), parent, num_segments=voxel_total)
    pooled = (summed / counts_flat.astype(jnp.float32)[:, None]).astype(jnp.bfloat16)
    coarse_in = jnp.zeros((voxel_total, C0), jnp.bfloat16).at[voxel_slot.astype(jnp.int32)].set(pooled)
    projected = project(coarse_in, w_pool)
    coarse = jax.nn.gelu(layer_norm(projected)).astype(jnp.bfloat16)
    normed2 = layer_norm(coarse).astype(jnp.bfloat16)
    query1 = project(normed2, w_query1).astype(jnp.bfloat16)
    key1 = project(normed2, w_key1).astype(jnp.bfloat16)
    value1 = project(normed2, w_value1).astype(jnp.bfloat16)
    zero_marks = jnp.zeros((PATCH,), jnp.int32)

    def level_one_block(block_index):
        start_row = (block_index * PATCH).astype(jnp.int32)
        queries = lax.dynamic_slice_in_dim(query1, start_row, PATCH, 0)
        key_rows = lax.dynamic_slice_in_dim(key1, start_row, PATCH, 0)
        value_rows = lax.dynamic_slice_in_dim(value1, start_row, PATCH, 0)
        return attend(queries, key_rows, value_rows, zero_marks, zero_marks)
    mixed1 = lax.map(level_one_block, jnp.arange(voxel_total // PATCH, dtype=jnp.int32))
    mixed1 = mixed1.reshape(voxel_total, C1)
    coarse_out = (coarse.astype(jnp.float32) + project(mixed1, w_attn_out1)).astype(jnp.bfloat16)
    lifted = project(coarse_out, w_up).astype(jnp.bfloat16)
    per_voxel = lifted[voxel_slot.astype(jnp.int32)]
    per_point = per_voxel[parent]
    refined = (fine.astype(jnp.float32) + per_point.astype(jnp.float32)).astype(jnp.bfloat16)
    return refined
```

```python
import functools

import jax
import jax.numpy as jnp
from jax import lax
from jax.experimental import pallas as pl
from jax.experimental.pallas import tpu as pltpu
from jax.sharding import PartitionSpec as P

HEAD = 16
PATCH = 1024
EPSILON = 1e-05
NEG_LARGE = -1e30
TILE = 256
SPAN = 384
HI_ROWS = 64
LO_ROWS = 128
OUTSIDE = 1 << 20
MESH = pl.DeviceIdType.MESH
BF16 = jnp.bfloat16
F32 = jnp.float32
VMEM = pl.BlockSpec(memory_space=pltpu.VMEM)
SMEM = pl.BlockSpec(memory_space=pltpu.SMEM)
VMEM_BYTES = 50 * 1024 * 1024

NN = (((1,), (0,)), ((), ()))
NT = (((1,), (1,)), ((), ()))
TN = (((0,), (0,)), ((), ()))


def dot(a, b, dims=NN):
    return lax.dot_general(a, b, dims, preferred_element_type=F32)


def norm(values):
    values = values.astype(F32)
    centre = values - jnp.mean(values, axis=0, keepdims=True)
    spread = jnp.mean(centre * centre, axis=0, keepdims=True)
    return centre * lax.rsqrt(spread + EPSILON)


def gelu(x):
    return 0.5 * x * (1.0 + jnp.tanh(0.7978845608028654 * (x + 0.044715 * (x * x * x))))


def greet(partners):
    barrier = pltpu.get_barrier_semaphore()
    for partner in partners:
        pl.semaphore_signal(barrier, inc=1, device_id=partner, device_id_type=MESH)
    pl.semaphore_wait(barrier, len(partners))


def remote(src, dst, sems, index, partner):
    send, recv = sems
    return pltpu.make_async_remote_copy(
        src_ref=src, dst_ref=dst, send_sem=send.at[index], recv_sem=recv.at[index],
        device_id=partner, device_id_type=MESH,
    )


def prologue_kernel(serial_count, level_count, points, marks, slots, q0, k0, v0, o0, m_in, m_out, q1, k1, v1, o1,
                    window, window_marks, slots_all, small, large, send, recv, local):
    s, l, f = lax.axis_index("serial"), lax.axis_index("level"), lax.axis_index("feat")
    other = 1 - f
    shard = s * level_count + l
    total = serial_count * level_count
    beside = lax.rem(shard + 2 * f - 1 + total, total)
    sibling = {"feat": other}
    edge = {"serial": beside // level_count, "level": lax.rem(beside, level_count), "feat": other}
    peers = [{"serial": lax.rem(s + d, serial_count)} for d in range(1, serial_count)]
    greet([sibling, edge] + peers)
    sems = (send, recv)
    rows = points.shape[1]
    kept = rows - PATCH
    src = pl.ds(pl.multiple_of(f * kept, PATCH), PATCH)
    dst = pl.ds(pl.multiple_of(other * kept, PATCH), PATCH)
    copies = [
        remote(points.at[:, src], window.at[:, dst], sems, 0, edge),
        remote(marks.at[:, src], window_marks.at[:, dst], sems, 1, edge),
    ]
    for copy in copies:
        copy.start()
    half = rows // 2 - PATCH
    near = pl.ds(pl.multiple_of(f * PATCH, PATCH), kept)
    here = pl.ds(pl.multiple_of(other * PATCH, PATCH), kept)
    own = [
        pltpu.make_async_copy(points.at[:, near], window.at[:, here], local.at[0]),
        pltpu.make_async_copy(marks.at[:, near], window_marks.at[:, here], local.at[1]),
    ]
    for copy in own:
        copy.start()
    for place, part in enumerate((q0, k0, v0, o0)):
        small[f, place] = part[...]
    for place, part in enumerate((m_in, m_out, q1, k1, v1, o1)):
        large[f, place] = part[...]
    weights = [
        remote(small.at[f], small.at[f], sems, 2, sibling),
        remote(large.at[f], large.at[f], sems, 3, sibling),
    ]
    for copy in weights:
        copy.start()
    slots_all[s] = slots[...]
    for d, peer in enumerate(peers):
        copy = remote(slots, slots_all.at[s], sems, 4 + d, peer)
        copy.start()
        copies.append(copy)
    for copy in own + copies + weights:
        copy.wait()


def swap_kernel(src, out, send, recv):
    f = lax.axis_index("feat")
    sibling = {"feat": 1 - f}
    greet([sibling])
    copy = remote(src, out.at[f], (send, recv), 0, sibling)
    copy.start()
    out[f] = src[...]
    copy.wait()


def gather_kernel(serial_count, src, out, send, recv):
    s, f = lax.axis_index("serial"), lax.axis_index("feat")
    sibling = {"feat": 1 - f}
    peers = [{"serial": lax.rem(s + d, serial_count)} for d in range(1, serial_count)]
    greet([sibling] + peers)
    sems = (send, recv)
    first = [remote(src, out.at[s, f], sems, d, peer) for d, peer in enumerate(peers)]
    for copy in first:
        copy.start()
    relays = [remote(src, out.at[s, f], sems, serial_count - 1, sibling)]
    relays[0].start()
    out[s, f] = src[...]
    for d, copy in enumerate(first):
        copy.wait_recv()
        origin = lax.rem(s + serial_count - d - 1, serial_count)
        relay = remote(out.at[origin, f], out.at[origin, f], sems, serial_count + d, sibling)
        relay.start()
        relays.append(relay)
    for copy in first:
        copy.wait_send()
    for copy in relays:
        copy.wait()


def fine_kernel(ranges, window, window_marks, small, large, out, keys, values_t, queries_t, scores):
    marks = window_marks[...]
    high = jnp.where((marks < 0) | (marks >= OUTSIDE), HI_ROWS - 1, marks // LO_ROWS)
    low = jnp.where(marks < 0, 0, marks % LO_ROWS)
    total = window.shape[1]
    count = out.shape[1]
    width = window.shape[0]
    heads = width // HEAD
    first = (total - count) // 2
    normed = norm(window[...]).astype(BF16)
    weight = [jnp.concatenate([small[0, i], small[1, i]], axis=0) for i in range(4)]
    queries_t[...] = (dot(weight[0], normed[:, first:first + count]).astype(BF16) * HEAD ** (-0.5)).astype(BF16)
    values_t[...] = dot(weight[2], normed).astype(BF16)
    key_t = dot(weight[1], normed).astype(BF16)
    for start in range(0, total, TILE):
        part = slice(start, start + TILE)
        hot_high = (lax.broadcasted_iota(jnp.int32, (HI_ROWS, TILE), 0) == high[:, part]).astype(F32)
        hot_low = (lax.broadcasted_iota(jnp.int32, (LO_ROWS, TILE), 0) == low[:, part]).astype(F32)
        stacked = jnp.concatenate([key_t[:, part].astype(F32), hot_high, hot_low], axis=0)
        keys[part, :] = jnp.transpose(stacked).astype(BF16)

    def block(index, carry):
        columns = pl.ds(pl.multiple_of(index * TILE, TILE), TILE)
        middle = pl.ds(pl.multiple_of(first + index * TILE, TILE), TILE)
        own = window_marks[:, middle]
        hot_high = lax.broadcasted_iota(jnp.int32, (HI_ROWS, TILE), 0) == own // LO_ROWS
        hot_low = lax.broadcasted_iota(jnp.int32, (LO_ROWS, TILE), 0) == own % LO_ROWS
        barred = jnp.concatenate(
            [jnp.where(hot_high, 0.0, NEG_LARGE), jnp.where(hot_low, 0.0, NEG_LARGE)], axis=0
        ).astype(BF16)
        query = queries_t[:, columns].astype(F32)
        head_of = lax.broadcasted_iota(jnp.int32, (width, TILE), 0) // HEAD
        asked = jnp.concatenate(
            [
                jnp.concatenate([jnp.where(head_of == h, query, 0.0).astype(BF16), barred], axis=0)
                for h in range(heads)
            ],
            axis=1,
        )
        low_tile, high_tile = ranges[2 * index], ranges[2 * index + 1]

        def score(tile, top):
            rows = pl.ds(pl.multiple_of(tile * TILE, TILE), TILE)
            got = dot(keys[rows, :], asked)
            scores[pl.ds(pl.multiple_of((tile - low_tile) * TILE, TILE), TILE), :] = got
            return jnp.maximum(top, jnp.max(got.reshape(TILE // 8, 8, heads * TILE), axis=0))

        top = lax.fori_loop(low_tile, high_tile, score, jnp.full((8, heads * TILE), -3e38, F32))
        top = jnp.max(top, axis=0, keepdims=True)

        def mix(tile, state):
            total_weight, sums = state
            rows = pl.ds(pl.multiple_of((tile - low_tile) * TILE, TILE), TILE)
            places = pl.ds(pl.multiple_of(tile * TILE, TILE), TILE)
            weights = jnp.exp(scores[rows, :] - top)
            total_weight = total_weight + jnp.sum(weights.reshape(TILE // 8, 8, heads * TILE), axis=0)
            rounded = weights.astype(BF16)
            sums = tuple(
                sums[h]
                + dot(values_t[h * HEAD:(h + 1) * HEAD, places], rounded[:, h * TILE:(h + 1) * TILE])
                for h in range(heads)
            )
            return total_weight, sums

        total_weight, sums = lax.fori_loop(
            low_tile, high_tile, mix,
            (jnp.zeros((8, heads * TILE), F32), tuple(jnp.zeros((HEAD, TILE), F32) for _ in range(heads))),
        )
        total_weight = jnp.sum(total_weight, axis=0, keepdims=True)
        mixed = jnp.concatenate(
            [sums[h] / total_weight[:, h * TILE:(h + 1) * TILE] for h in range(heads)], axis=0
        ).astype(BF16)
        hidden = (window[:, middle].astype(F32) + dot(weight[3], mixed, TN)).astype(BF16)
        normed1 = norm(hidden).astype(BF16)
        fed = jnp.zeros((width, TILE), F32)
        for f in range(2):
            inner = gelu(dot(large[f, 0], normed1, TN)).astype(BF16)
            fed = fed + dot(large[f, 1], inner)
        out[:, columns] = (hidden.astype(F32) + fed).astype(BF16)
        return carry

    lax.fori_loop(0, count // TILE, block, 0)


def belongs(starts, ends, offset):
    places = lax.broadcasted_iota(jnp.int32, (TILE, SPAN), 0) + offset
    return jnp.where((places >= starts) & (places < ends), 1.0, 0.0).astype(BF16)


def pool_kernel(lows, fine, starts, ends, out, sums):
    sums[...] = jnp.zeros_like(sums)
    half = fine.shape[2]
    for index in range(2 * half // TILE):
        start = index * TILE
        near = pl.ds(pl.multiple_of(lows[index] * 128, 128), SPAN)
        owner = belongs(starts[:, near], ends[:, near], start)
        block = fine[start // half, :, start % half:start % half + TILE]
        sums[:, near] += dot(block, owner)
    rows = out.shape[1]
    mine = pl.ds(pl.multiple_of(lax.axis_index("feat") * rows, 128), rows)
    members = (ends[:, mine] - starts[:, mine]).astype(F32)
    out[...] = (sums[:, mine] / members).astype(BF16)


def coarse_kernel(serial_count, level_count, pooled, slots, large, w_pool, w_up, out, landed, keys, queries_t, values_t):
    s, l, f = lax.axis_index("serial"), lax.axis_index("level"), lax.axis_index("feat")
    count = out.shape[1]
    base = ((s * level_count + l) * 2 + f) * count
    row = lax.broadcasted_iota(jnp.int32, (TILE, count), 0)

    def land(index, carry):
        columns = pl.ds(pl.multiple_of(index * TILE, TILE), TILE)
        total = jnp.zeros((out.shape[0], TILE), F32)
        for origin in range(serial_count):
            for half in range(2):
                asked = slots[origin, :, half * count:(half + 1) * count] - (base + index * TILE)
                chosen = jnp.where(asked == row, 1.0, 0.0).astype(BF16)
                total = total + dot(pooled[origin, half], chosen, NT)
        landed[:, columns] = total.astype(BF16)
        return carry

    lax.fori_loop(0, count // TILE, land, 0)
    coarse = gelu(norm(dot(w_pool[...], landed[...], TN))).astype(BF16)
    normed = norm(coarse).astype(BF16)
    weight = [jnp.concatenate([large[0, i], large[1, i]], axis=0) for i in range(2, 6)]
    width = coarse.shape[0]
    heads = width // HEAD
    queries_t[...] = (dot(weight[0], normed).astype(BF16) * HEAD ** (-0.5)).astype(BF16)
    values_t[...] = dot(weight[2], normed).astype(BF16)
    keys[...] = jnp.transpose(dot(weight[1], normed)).astype(BF16)
    head_of = lax.broadcasted_iota(jnp.int32, (width, TILE), 0) // HEAD
    for start in range(0, count, TILE):
        part = slice(start, start + TILE)
        query = queries_t[:, part].astype(F32)
        parts = []
        for h in range(heads):
            got = dot(keys[...], jnp.where(head_of == h, query, 0.0).astype(BF16))
            weights = jnp.exp(got - jnp.max(got, axis=0, keepdims=True))
            total = jnp.sum(weights, axis=0, keepdims=True)
            parts.append(dot(values_t[h * HEAD:(h + 1) * HEAD, :], weights.astype(BF16)) / total)
        mixed = jnp.concatenate(parts, axis=0).astype(BF16)
        done = (coarse[:, part].astype(F32) + dot(weight[3], mixed, TN)).astype(BF16)
        out[:, part] = dot(w_up[...], done).astype(BF16)


def spread_kernel(serial_count, level_count, lows, lifted, slots, fine, starts, ends, out, nearby):
    l = lax.axis_index("level")
    count = lifted.shape[3]
    row = lax.broadcasted_iota(jnp.int32, (count, TILE), 0)

    def fetch(index, carry):
        columns = pl.ds(pl.multiple_of(index * TILE, TILE), TILE)
        wanted = slots[:, columns]
        total = jnp.zeros((out.shape[0], TILE), F32)
        for origin in range(serial_count):
            for half in range(2):
                base = ((origin * level_count + l) * 2 + half) * count
                chosen = jnp.where(wanted - base == row, 1.0, 0.0).astype(BF16)
                total = total + dot(lifted[origin, half], chosen)
        nearby[:, columns] = total.astype(BF16)
        return carry

    lax.fori_loop(0, slots.shape[1] // TILE, fetch, 0)
    half = fine.shape[2]
    for index in range(2 * half // TILE):
        start = index * TILE
        near = pl.ds(pl.multiple_of(lows[index] * 128, 128), SPAN)
        owner = belongs(starts[:, near], ends[:, near], start)
        block = fine[start // half, :, start % half:start % half + TILE]
        out[:, start:start + TILE] = (block.astype(F32) + dot(nearby[:, near], owner, NT)).astype(BF16)


def call(kernel, outs, ins, scratch=(), collective=None):
    params = dict(vmem_limit_bytes=VMEM_BYTES)
    if collective is not None:
        params.update(collective_id=collective, has_side_effects=True)
    return pl.pallas_call(
        kernel,
        out_shape=[jax.ShapeDtypeStruct(shape, kind) for shape, kind in outs],
        in_specs=[SMEM if place == "scalar" else VMEM for place, _ in ins],
        out_specs=[VMEM] * len(outs),
        scratch_shapes=list(scratch),
        compiler_params=pltpu.CompilerParams(**params),
    )(*[value for _, value in ins])


def vectors(*values):
    return [("vector", value) for value in values]


def local(points, patch_ids, child_counts, voxel_slot, w_query0, w_key0, w_value0, w_attn_out0, w_mlp_in, w_mlp_out,
          w_pool, w_query1, w_key1, w_value1, w_attn_out1, w_up):
    rows, width = points.shape
    voxels = voxel_slot.shape[0]
    serial_count, level_count = lax.axis_size("serial"), lax.axis_size("level")
    dma = pltpu.SemaphoreType.DMA
    slots = voxel_slot.reshape(1, voxels)
    counts = child_counts.reshape(1, voxels)
    ends = jnp.cumsum(counts, axis=1)
    starts = ends - counts
    tiles = jnp.arange(rows // TILE, dtype=jnp.int32) * TILE
    lows = jnp.minimum(jnp.sum((ends <= tiles[:, None]).astype(jnp.int32), axis=1) // 128, (voxels - SPAN) // 128)

    window, window_marks, slots_all, small, large = call(
        functools.partial(prologue_kernel, serial_count, level_count),
        [
            ((width, rows), BF16), ((1, rows), jnp.int32), ((serial_count, 1, voxels), jnp.int32),
            ((2, 4) + w_query0.shape[::-1], BF16), ((2, 6) + w_mlp_in.shape, BF16),
        ],
        vectors(points.T, patch_ids.reshape(1, rows), slots, w_query0.T, w_key0.T, w_value0.T, w_attn_out0,
                w_mlp_in, w_mlp_out.T, w_query1.T, w_key1.T, w_value1.T, w_attn_out1),
        [dma((3 + serial_count,)), dma((3 + serial_count,)), dma((2,))],
        collective=0,
    )
    shard = lax.axis_index("serial") * level_count + lax.axis_index("level")
    f = lax.axis_index("feat")
    place = jnp.arange(rows, dtype=jnp.int32)[None, :]
    before = (shard == 0) & (f == 0) & (place < PATCH)
    after = (shard == serial_count * level_count - 1) & (f == 1) & (place >= rows - PATCH)
    window_marks = jnp.where(before, -1, jnp.where(after, OUTSIDE, window_marks))
    half = rows // 2
    asked = window_marks[0, half // 2:half // 2 + half].reshape(-1, TILE)
    low = jnp.sum((window_marks < asked[:, :1]).astype(jnp.int32), axis=1) // TILE
    high = (jnp.sum((window_marks <= asked[:, -1:]).astype(jnp.int32), axis=1) + TILE - 1) // TILE
    ranges = jnp.stack([low, high], axis=1).reshape(-1)

    (fine_half,) = call(
        fine_kernel,
        [((width, half), BF16)],
        [("scalar", ranges)] + vectors(window, window_marks, small, large),
        [
            pltpu.VMEM((rows, width + HI_ROWS + LO_ROWS), BF16), pltpu.VMEM((width, rows), BF16),
            pltpu.VMEM((width, half), BF16), pltpu.VMEM((2 * PATCH + TILE, width // HEAD * TILE), F32),
        ],
    )
    (fine,) = call(swap_kernel, [((2, width, half), BF16)], vectors(fine_half), [dma((1,)), dma((1,))], collective=1)
    part = voxels // 2
    (pooled_part,) = call(
        pool_kernel,
        [((width, part), BF16)],
        [("scalar", lows)] + vectors(fine, starts, ends),
        [pltpu.VMEM((width, voxels), F32)],
    )

    def gathered(value, collective):
        sems = dma((2 * serial_count - 1,))
        (result,) = call(
            functools.partial(gather_kernel, serial_count),
            [((serial_count, 2) + value.shape, value.dtype)], vectors(value), [sems, sems], collective=collective,
        )
        return result

    pooled = gathered(pooled_part, 2)
    wide = w_pool.shape[1]
    (lifted_part,) = call(
        functools.partial(coarse_kernel, serial_count, level_count),
        [((width, part), BF16)],
        vectors(pooled, slots_all, large, w_pool, w_up.T),
        [
            pltpu.VMEM((width, part), BF16), pltpu.VMEM((part, wide), BF16),
            pltpu.VMEM((wide, part), BF16), pltpu.VMEM((wide, part), BF16),
        ],
    )
    lifted = gathered(lifted_part, 3)
    (refined,) = call(
        functools.partial(spread_kernel, serial_count, level_count),
        [((width, rows), BF16)],
        [("scalar", lows)] + vectors(lifted, slots, fine, starts, ends),
        [pltpu.VMEM((width, voxels), BF16)],
    )
    return refined.T


def solution(mesh):
    shards = ("groups", "serial", "level")
    columns, stacked = P(None, "feat"), P("feat", None)
    in_specs = (
        P(shards, None), P(shards), P(shards, None), P(shards),
        columns, columns, columns, stacked, columns, stacked, P(),
        columns, columns, columns, stacked, P(),
    )
    return jax.shard_map(local, mesh=mesh, in_specs=in_specs, out_specs=P(shards, None), check_vma=False)
```

```python
import functools

import jax
import jax.numpy as jnp
from jax import lax
from jax.experimental import pallas as pl
from jax.experimental.pallas import tpu as pltpu
from jax.sharding import PartitionSpec as P

HEAD = 16
PATCH = 1024
EPSILON = 1e-05
NEG_LARGE = -1e30
TILE = 256
SPAN = 384
HI_ROWS = 64
LO_ROWS = 128
OUTSIDE = 1 << 20
MESH = pl.DeviceIdType.MESH
BF16 = jnp.bfloat16
F32 = jnp.float32
VMEM = pl.BlockSpec(memory_space=pltpu.VMEM)
SMEM = pl.BlockSpec(memory_space=pltpu.SMEM)
VMEM_BYTES = 50 * 1024 * 1024

NN = (((1,), (0,)), ((), ()))
NT = (((1,), (1,)), ((), ()))
TN = (((0,), (0,)), ((), ()))


def dot(a, b, dims=NN):
    return lax.dot_general(a, b, dims, preferred_element_type=F32)


def norm(values):
    values = values.astype(F32)
    centre = values - jnp.mean(values, axis=0, keepdims=True)
    spread = jnp.mean(centre * centre, axis=0, keepdims=True)
    return centre * lax.rsqrt(spread + EPSILON)


def gelu(x):
    return 0.5 * x * (1.0 + jnp.tanh(0.7978845608028654 * (x + 0.044715 * (x * x * x))))


def greet(partners):
    barrier = pltpu.get_barrier_semaphore()
    for partner in partners:
        pl.semaphore_signal(barrier, inc=1, device_id=partner, device_id_type=MESH)
    pl.semaphore_wait(barrier, len(partners))


def remote(src, dst, sems, index, partner):
    send, recv = sems
    return pltpu.make_async_remote_copy(
        src_ref=src, dst_ref=dst, send_sem=send.at[index], recv_sem=recv.at[index],
        device_id=partner, device_id_type=MESH,
    )


def prologue_kernel(serial_count, level_count, points, marks, slots, q0, k0, v0, o0, m_in, m_out, q1, k1, v1, o1,
                    window, window_marks, slots_all, small, large, send, recv, local):
    s, l, f = lax.axis_index("serial"), lax.axis_index("level"), lax.axis_index("feat")
    other = 1 - f
    shard = s * level_count + l
    total = serial_count * level_count
    beside = lax.rem(shard + 2 * f - 1 + total, total)
    sibling = {"feat": other}
    edge = {"serial": beside // level_count, "level": lax.rem(beside, level_count), "feat": other}
    peers = [{"serial": lax.rem(s + d, serial_count)} for d in range(1, serial_count)]
    greet([sibling, edge] + peers)
    sems = (send, recv)
    rows = points.shape[1]
    kept = rows - PATCH
    src = pl.ds(pl.multiple_of(f * kept, PATCH), PATCH)
    dst = pl.ds(pl.multiple_of(other * kept, PATCH), PATCH)
    copies = [
        remote(points.at[:, src], window.at[:, dst], sems, 0, edge),
        remote(marks.at[:, src], window_marks.at[:, dst], sems, 1, edge),
    ]
    for copy in copies:
        copy.start()
    near = pl.ds(pl.multiple_of(f * PATCH, PATCH), kept)
    here = pl.ds(pl.multiple_of(other * PATCH, PATCH), kept)
    own = [
        pltpu.make_async_copy(points.at[:, near], window.at[:, here], local.at[0]),
        pltpu.make_async_copy(marks.at[:, near], window_marks.at[:, here], local.at[1]),
    ]
    for copy in own:
        copy.start()
    for place, part in enumerate((q0, k0, v0, o0)):
        small[f, place] = part[...]
    for place, part in enumerate((m_in, m_out, q1, k1, v1, o1)):
        large[f, place] = part[...]
    weights = [
        remote(small.at[f], small.at[f], sems, 2, sibling),
        remote(large.at[f], large.at[f], sems, 3, sibling),
    ]
    for copy in weights:
        copy.start()
    slots_all[s] = slots[...]
    for d, peer in enumerate(peers):
        copy = remote(slots, slots_all.at[s], sems, 4 + d, peer)
        copy.start()
        copies.append(copy)
    for copy in own + copies + weights:
        copy.wait()


def swap_kernel(src, out, send, recv):
    f = lax.axis_index("feat")
    sibling = {"feat": 1 - f}
    greet([sibling])
    copy = remote(src, out.at[f], (send, recv), 0, sibling)
    copy.start()
    out[f] = src[...]
    copy.wait()


def fine_kernel(ranges, window, window_marks, small, large, out, keys, values_t, queries_t, scores):
    marks = window_marks[...]
    high = jnp.where((marks < 0) | (marks >= OUTSIDE), HI_ROWS - 1, marks // LO_ROWS)
    low = jnp.where(marks < 0, 0, marks % LO_ROWS)
    total = window.shape[1]
    count = out.shape[1]
    width = window.shape[0]
    heads = width // HEAD
    first = (total - count) // 2
    normed = norm(window[...]).astype(BF16)
    weight = [jnp.concatenate([small[0, i], small[1, i]], axis=0) for i in range(4)]
    queries_t[...] = (dot(weight[0], normed[:, first:first + count]).astype(BF16) * HEAD ** (-0.5)).astype(BF16)
    values_t[...] = dot(weight[2], normed).astype(BF16)
    key_t = dot(weight[1], normed).astype(BF16)
    for start in range(0, total, TILE):
        part = slice(start, start + TILE)
        hot_high = (lax.broadcasted_iota(jnp.int32, (HI_ROWS, TILE), 0) == high[:, part]).astype(F32)
        hot_low = (lax.broadcasted_iota(jnp.int32, (LO_ROWS, TILE), 0) == low[:, part]).astype(F32)
        stacked = jnp.concatenate([key_t[:, part].astype(F32), hot_high, hot_low], axis=0)
        keys[part, :] = jnp.transpose(stacked).astype(BF16)

    def block(index, carry):
        columns = pl.ds(pl.multiple_of(index * TILE, TILE), TILE)
        middle = pl.ds(pl.multiple_of(first + index * TILE, TILE), TILE)
        own = window_marks[:, middle]
        hot_high = lax.broadcasted_iota(jnp.int32, (HI_ROWS, TILE), 0) == own // LO_ROWS
        hot_low = lax.broadcasted_iota(jnp.int32, (LO_ROWS, TILE), 0) == own % LO_ROWS
        barred = jnp.concatenate(
            [jnp.where(hot_high, 0.0, NEG_LARGE), jnp.where(hot_low, 0.0, NEG_LARGE)], axis=0
        ).astype(BF16)
        query = queries_t[:, columns].astype(F32)
        head_of = lax.broadcasted_iota(jnp.int32, (width, TILE), 0) // HEAD
        asked = jnp.concatenate(
            [
                jnp.concatenate([jnp.where(head_of == h, query, 0.0).astype(BF16), barred], axis=0)
                for h in range(heads)
            ],
            axis=1,
        )
        low_tile, high_tile = ranges[2 * index], ranges[2 * index + 1]

        def score(tile, top):
            rows = pl.ds(pl.multiple_of(tile * TILE, TILE), TILE)
            got = dot(keys[rows, :], asked)
            scores[pl.ds(pl.multiple_of((tile - low_tile) * TILE, TILE), TILE), :] = got
            return jnp.maximum(top, jnp.max(got.reshape(TILE // 8, 8, heads * TILE), axis=0))

        top = lax.fori_loop(low_tile, high_tile, score, jnp.full((8, heads * TILE), -3e38, F32))
        top = jnp.max(top, axis=0, keepdims=True)

        def mix(tile, state):
            total_weight, sums = state
            rows = pl.ds(pl.multiple_of((tile - low_tile) * TILE, TILE), TILE)
            places = pl.ds(pl.multiple_of(tile * TILE, TILE), TILE)
            weights = jnp.exp(scores[rows, :] - top)
            total_weight = total_weight + jnp.sum(weights.reshape(TILE // 8, 8, heads * TILE), axis=0)
            rounded = weights.astype(BF16)
            sums = tuple(
                sums[h]
                + dot(values_t[h * HEAD:(h + 1) * HEAD, places], rounded[:, h * TILE:(h + 1) * TILE])
                for h in range(heads)
            )
            return total_weight, sums

        total_weight, sums = lax.fori_loop(
            low_tile, high_tile, mix,
            (jnp.zeros((8, heads * TILE), F32), tuple(jnp.zeros((HEAD, TILE), F32) for _ in range(heads))),
        )
        total_weight = jnp.sum(total_weight, axis=0, keepdims=True)
        mixed = jnp.concatenate(
            [sums[h] / total_weight[:, h * TILE:(h + 1) * TILE] for h in range(heads)], axis=0
        ).astype(BF16)
        hidden = (window[:, middle].astype(F32) + dot(weight[3], mixed, TN)).astype(BF16)
        normed1 = norm(hidden).astype(BF16)
        fed = jnp.zeros((width, TILE), F32)
        for f in range(2):
            inner = gelu(dot(large[f, 0], normed1, TN)).astype(BF16)
            fed = fed + dot(large[f, 1], inner)
        out[:, columns] = (hidden.astype(F32) + fed).astype(BF16)
        return carry

    lax.fori_loop(0, count // TILE, block, 0)


def belongs(starts, ends, offset):
    places = lax.broadcasted_iota(jnp.int32, (TILE, SPAN), 0) + offset
    return jnp.where((places >= starts) & (places < ends), 1.0, 0.0).astype(BF16)


def pool_kernel(lows, fine, starts, ends, out, sums):
    sums[...] = jnp.zeros_like(sums)
    half = fine.shape[2]
    for index in range(2 * half // TILE):
        start = index * TILE
        near = pl.ds(pl.multiple_of(lows[index] * 128, 128), SPAN)
        owner = belongs(starts[:, near], ends[:, near], start)
        block = fine[start // half, :, start % half:start % half + TILE]
        sums[:, near] += dot(block, owner)
    rows = out.shape[1]
    mine = pl.ds(pl.multiple_of(lax.axis_index("feat") * rows, 128), rows)
    members = (ends[:, mine] - starts[:, mine]).astype(F32)
    out[...] = (sums[:, mine] / members).astype(BF16)


def coarse_kernel(serial_count, level_count, part, slots_all, own_slots, large, w_pool, w_up, out,
                  pooled, lifted, landed, keys, queries_t, values_t, nearby, send1, recv1, send2, recv2):
    s, l, f = lax.axis_index("serial"), lax.axis_index("level"), lax.axis_index("feat")
    other = 1 - f
    sibling = {"feat": other}
    peers = [{"serial": lax.rem(s + d, serial_count)} for d in range(1, serial_count)]
    origins = [lax.rem(s + serial_count - d, serial_count) for d in range(serial_count)]
    greet([sibling] + peers)
    count = part.shape[1]
    blocks = count // TILE

    def share(source, slot, send, recv, first):
        sems = (send, recv)
        copies = [remote(source, slot, sems, first, sibling)]
        copies += [remote(source, slot, sems, first + d, peer) for d, peer in enumerate(peers, 1)]
        for copy in copies[1:] + copies[:1]:
            copy.start()
        return copies

    def relay(slot, send, recv, index):
        copy = remote(slot, slot, (send, recv), index, sibling)
        copy.start()
        return copy

    copies = share(part, pooled.at[s, f], send1, recv1, 0)
    pooled[s, f] = part[...]
    base = ((s * level_count + l) * 2 + f) * count
    row = lax.broadcasted_iota(jnp.int32, (TILE, count), 0)
    landed[...] = jnp.zeros_like(landed)

    def land(origin, half):
        values = pooled[origin, half]
        columns = pl.ds(pl.multiple_of(half * count, TILE), count)
        wanted = slots_all[origin, :, columns] - base
        for index in range(blocks):
            chosen = jnp.where(wanted - index * TILE == row, 1.0, 0.0).astype(BF16)
            landed[:, index * TILE:(index + 1) * TILE] += dot(values, chosen, NT)

    land(s, f)
    copies[0].wait_recv()
    land(s, other)
    relays = []
    for d in range(1, serial_count):
        copies[d].wait_recv()
        relays.append(relay(pooled.at[origins[d], f], send1, recv1, serial_count + d - 1))
        land(origins[d], f)
        if d > 1:
            relays[d - 2].wait_recv()
            land(origins[d - 1], other)
    if relays:
        relays[-1].wait_recv()
        land(origins[-1], other)
    for copy in copies + relays:
        copy.wait_send()

    coarse = gelu(norm(dot(w_pool[...], landed[...].astype(BF16), TN))).astype(BF16)
    normed = norm(coarse).astype(BF16)
    weight = [jnp.concatenate([large[0, i], large[1, i]], axis=0) for i in range(2, 6)]
    width = coarse.shape[0]
    heads = width // HEAD
    queries_t[...] = (dot(weight[0], normed).astype(BF16) * HEAD ** (-0.5)).astype(BF16)
    values_t[...] = dot(weight[2], normed).astype(BF16)
    keys[...] = jnp.transpose(dot(weight[1], normed)).astype(BF16)
    head_of = lax.broadcasted_iota(jnp.int32, (width, TILE), 0) // HEAD
    stride = 2 * serial_count - 1
    sent, passed = [], []

    def forward(block):
        got = []
        for d in range(1, serial_count):
            sent[block][d].wait_recv()
            got.append(relay(lifted.at[origins[d], f, block], send2, recv2, block * stride + serial_count + d - 1))
        passed.append(got)

    for block in range(blocks):
        columns = slice(block * TILE, (block + 1) * TILE)
        query = queries_t[:, columns].astype(F32)
        parts = []
        for h in range(heads):
            got = dot(keys[...], jnp.where(head_of == h, query, 0.0).astype(BF16))
            weights = jnp.exp(got - jnp.max(got, axis=0, keepdims=True))
            total = jnp.sum(weights, axis=0, keepdims=True)
            parts.append(dot(values_t[h * HEAD:(h + 1) * HEAD, :], weights.astype(BF16)) / total)
        mixed = jnp.concatenate(parts, axis=0).astype(BF16)
        done = (coarse[:, columns].astype(F32) + dot(weight[3], mixed, TN)).astype(BF16)
        lifted[s, f, block] = dot(w_up[...], done).astype(BF16)
        slot = lifted.at[s, f, block]
        sent.append(share(slot, slot, send2, recv2, block * stride))
        if block > 0:
            forward(block - 1)

    nearby[...] = jnp.zeros_like(nearby)
    square = lax.broadcasted_iota(jnp.int32, (TILE, TILE), 0)

    def arrived(block):
        sent[block][0].wait_recv()
        for copy in passed[block]:
            copy.wait_recv()

    def fetch(chosen_blocks):
        def column(index, carry):
            columns = pl.ds(pl.multiple_of(index * TILE, TILE), TILE)
            wanted = own_slots[:, columns]
            total = nearby[:, columns]
            for origin in range(serial_count):
                for half in range(2):
                    start = ((origin * level_count + l) * 2 + half) * count
                    for block in chosen_blocks:
                        chosen = jnp.where(wanted - (start + block * TILE) == square, 1.0, 0.0).astype(BF16)
                        total = total + dot(lifted[origin, half, block], chosen)
            nearby[:, columns] = total
            return carry

        lax.fori_loop(0, own_slots.shape[1] // TILE, column, 0)

    for block in range(blocks - 2):
        arrived(block)
    fetch(range(blocks - 2))
    forward(blocks - 1)
    arrived(blocks - 2)
    fetch([blocks - 2])
    arrived(blocks - 1)
    fetch([blocks - 1])
    out[...] = nearby[...].astype(BF16)
    for group in sent + passed:
        for copy in group:
            copy.wait_send()


def spread_kernel(lows, nearby, fine, starts, ends, out):
    half = fine.shape[2]
    for index in range(2 * half // TILE):
        start = index * TILE
        near = pl.ds(pl.multiple_of(lows[index] * 128, 128), SPAN)
        owner = belongs(starts[:, near], ends[:, near], start)
        block = fine[start // half, :, start % half:start % half + TILE]
        out[:, start:start + TILE] = (block.astype(F32) + dot(nearby[:, near], owner, NT)).astype(BF16)


def call(kernel, outs, ins, scratch=(), collective=None):
    params = dict(vmem_limit_bytes=VMEM_BYTES)
    if collective is not None:
        params.update(collective_id=collective, has_side_effects=True)
    return pl.pallas_call(
        kernel,
        out_shape=[jax.ShapeDtypeStruct(shape, kind) for shape, kind in outs],
        in_specs=[SMEM if place == "scalar" else VMEM for place, _ in ins],
        out_specs=[VMEM] * len(outs),
        scratch_shapes=list(scratch),
        compiler_params=pltpu.CompilerParams(**params),
    )(*[value for _, value in ins])


def vectors(*values):
    return [("vector", value) for value in values]


def local(points, patch_ids, child_counts, voxel_slot, w_query0, w_key0, w_value0, w_attn_out0, w_mlp_in, w_mlp_out,
          w_pool, w_query1, w_key1, w_value1, w_attn_out1, w_up):
    rows, width = points.shape
    voxels = voxel_slot.shape[0]
    serial_count, level_count = lax.axis_size("serial"), lax.axis_size("level")
    dma = pltpu.SemaphoreType.DMA
    slots = voxel_slot.reshape(1, voxels)
    counts = child_counts.reshape(1, voxels)
    ends = jnp.cumsum(counts, axis=1)
    starts = ends - counts
    tiles = jnp.arange(rows // TILE, dtype=jnp.int32) * TILE
    lows = jnp.minimum(jnp.sum((ends <= tiles[:, None]).astype(jnp.int32), axis=1) // 128, (voxels - SPAN) // 128)

    window, window_marks, slots_all, small, large = call(
        functools.partial(prologue_kernel, serial_count, level_count),
        [
            ((width, rows), BF16), ((1, rows), jnp.int32), ((serial_count, 1, voxels), jnp.int32),
            ((2, 4) + w_query0.shape[::-1], BF16), ((2, 6) + w_mlp_in.shape, BF16),
        ],
        vectors(points.T, patch_ids.reshape(1, rows), slots, w_query0.T, w_key0.T, w_value0.T, w_attn_out0,
                w_mlp_in, w_mlp_out.T, w_query1.T, w_key1.T, w_value1.T, w_attn_out1),
        [dma((3 + serial_count,)), dma((3 + serial_count,)), dma((2,))],
        collective=0,
    )
    shard = lax.axis_index("serial") * level_count + lax.axis_index("level")
    f = lax.axis_index("feat")
    place = jnp.arange(rows, dtype=jnp.int32)[None, :]
    before = (shard == 0) & (f == 0) & (place < PATCH)
    after = (shard == serial_count * level_count - 1) & (f == 1) & (place >= rows - PATCH)
    window_marks = jnp.where(before, -1, jnp.where(after, OUTSIDE, window_marks))
    half = rows // 2
    asked = window_marks[0, half // 2:half // 2 + half].reshape(-1, TILE)
    low = jnp.sum((window_marks < asked[:, :1]).astype(jnp.int32), axis=1) // TILE
    high = (jnp.sum((window_marks <= asked[:, -1:]).astype(jnp.int32), axis=1) + TILE - 1) // TILE
    ranges = jnp.stack([low, high], axis=1).reshape(-1)

    (fine_half,) = call(
        fine_kernel,
        [((width, half), BF16)],
        [("scalar", ranges)] + vectors(window, window_marks, small, large),
        [
            pltpu.VMEM((rows, width + HI_ROWS + LO_ROWS), BF16), pltpu.VMEM((width, rows), BF16),
            pltpu.VMEM((width, half), BF16), pltpu.VMEM((2 * PATCH + TILE, width // HEAD * TILE), F32),
        ],
    )
    (fine,) = call(swap_kernel, [((2, width, half), BF16)], vectors(fine_half), [dma((1,)), dma((1,))], collective=1)
    part = voxels // 2
    (pooled_part,) = call(
        pool_kernel,
        [((width, part), BF16)],
        [("scalar", lows)] + vectors(fine, starts, ends),
        [pltpu.VMEM((width, voxels), F32)],
    )

    wide = w_pool.shape[1]
    blocks = part // TILE
    each = 2 * serial_count - 1
    (nearby,) = call(
        functools.partial(coarse_kernel, serial_count, level_count),
        [((width, voxels), BF16)],
        vectors(pooled_part, slots_all, slots, large, w_pool, w_up.T),
        [
            pltpu.VMEM((serial_count, 2, width, part), BF16), pltpu.VMEM((serial_count, 2, blocks, width, TILE), BF16),
            pltpu.VMEM((width, part), F32), pltpu.VMEM((part, wide), BF16),
            pltpu.VMEM((wide, part), BF16), pltpu.VMEM((wide, part), BF16), pltpu.VMEM((width, voxels), F32),
            dma((each,)), dma((each,)), dma((blocks * each,)), dma((blocks * each,)),
        ],
        collective=2,
    )
    (refined,) = call(
        spread_kernel,
        [((width, rows), BF16)],
        [("scalar", lows)] + vectors(nearby, fine, starts, ends),
    )
    return refined.T


def solution(mesh):
    shards = ("groups", "serial", "level")
    columns, stacked = P(None, "feat"), P("feat", None)
    in_specs = (
        P(shards, None), P(shards), P(shards, None), P(shards),
        columns, columns, columns, stacked, columns, stacked, P(),
        columns, columns, columns, stacked, P(),
    )
    return jax.shard_map(local, mesh=mesh, in_specs=in_specs, out_specs=P(shards, None), check_vma=False)
```

```python
import functools

import jax
import jax.numpy as jnp
from jax import lax
from jax.experimental import pallas as pl
from jax.experimental.pallas import tpu as pltpu
from jax.sharding import PartitionSpec as P

HEAD = 16
PATCH = 1024
EPSILON = 1e-05
NEG_LARGE = -1e30
TILE = 256
SPAN = 384
HI_ROWS = 64
LO_ROWS = 64
BOUND = 64.0
UNIT = 1.4426950408889634 * HEAD ** (-0.5)
VALUE_ROWS = 2 * HEAD
OUTSIDE = 1 << 20
MESH = pl.DeviceIdType.MESH
BF16 = jnp.bfloat16
F32 = jnp.float32
VMEM = pl.BlockSpec(memory_space=pltpu.VMEM)
SMEM = pl.BlockSpec(memory_space=pltpu.SMEM)
VMEM_BYTES = 50 * 1024 * 1024

NN = (((1,), (0,)), ((), ()))
NT = (((1,), (1,)), ((), ()))
TN = (((0,), (0,)), ((), ()))


def dot(a, b, dims=NN):
    return lax.dot_general(a, b, dims, preferred_element_type=F32)


def norm(values):
    values = values.astype(F32)
    centre = values - jnp.mean(values, axis=0, keepdims=True)
    spread = jnp.mean(centre * centre, axis=0, keepdims=True)
    return centre * lax.rsqrt(spread + EPSILON)


def gelu(x):
    return 0.5 * x * (1.0 + jnp.tanh(0.7978845608028654 * (x + 0.044715 * (x * x * x))))


def in_parts(query, kept, factor):
    scaled = jnp.where(kept, query.astype(F32) * factor, 0.0)
    high = scaled.astype(BF16)
    return [high, (scaled - high.astype(F32)).astype(BF16)]


def with_ones(values, head):
    own = values[head * HEAD:(head + 1) * HEAD, :]
    extra = (lax.broadcasted_iota(jnp.int32, own.shape, 0) == 0).astype(BF16)
    return [own, extra]


def greet(partners):
    barrier = pltpu.get_barrier_semaphore()
    for partner in partners:
        pl.semaphore_signal(barrier, inc=1, device_id=partner, device_id_type=MESH)
    pl.semaphore_wait(barrier, len(partners))


def remote(src, dst, sems, index, partner):
    send, recv = sems
    return pltpu.make_async_remote_copy(
        src_ref=src, dst_ref=dst, send_sem=send.at[index], recv_sem=recv.at[index],
        device_id=partner, device_id_type=MESH,
    )


def prologue_kernel(serial_count, level_count, points, marks, slots, q0, k0, v0, o0, m_in, m_out, q1, k1, v1, o1,
                    window, window_marks, slots_all, small, large, send, recv, local):
    s, l, f = lax.axis_index("serial"), lax.axis_index("level"), lax.axis_index("feat")
    other = 1 - f
    shard = s * level_count + l
    total = serial_count * level_count
    beside = lax.rem(shard + 2 * f - 1 + total, total)
    sibling = {"feat": other}
    edge = {"serial": beside // level_count, "level": lax.rem(beside, level_count), "feat": other}
    peers = [{"serial": lax.rem(s + d, serial_count)} for d in range(1, serial_count)]
    greet([sibling, edge] + peers)
    sems = (send, recv)
    rows = points.shape[1]
    kept = rows - PATCH
    src = pl.ds(pl.multiple_of(f * kept, PATCH), PATCH)
    dst = pl.ds(pl.multiple_of(other * kept, PATCH), PATCH)
    copies = [
        remote(points.at[:, src], window.at[:, dst], sems, 0, edge),
        remote(marks.at[:, src], window_marks.at[:, dst], sems, 1, edge),
    ]
    for copy in copies:
        copy.start()
    near = pl.ds(pl.multiple_of(f * PATCH, PATCH), kept)
    here = pl.ds(pl.multiple_of(other * PATCH, PATCH), kept)
    own = [
        pltpu.make_async_copy(points.at[:, near], window.at[:, here], local.at[0]),
        pltpu.make_async_copy(marks.at[:, near], window_marks.at[:, here], local.at[1]),
    ]
    for copy in own:
        copy.start()
    for place, part in enumerate((q0, k0, v0, o0)):
        small[f, place] = part[...]
    for place, part in enumerate((m_in, m_out, q1, k1, v1, o1)):
        large[f, place] = part[...]
    weights = [
        remote(small.at[f], small.at[f], sems, 2, sibling),
        remote(large.at[f], large.at[f], sems, 3, sibling),
    ]
    for copy in weights:
        copy.start()
    slots_all[s] = slots[...]
    for d, peer in enumerate(peers):
        copy = remote(slots, slots_all.at[s], sems, 4 + d, peer)
        copy.start()
        copies.append(copy)
    for copy in own + copies + weights:
        copy.wait()


def swap_kernel(src, out, send, recv):
    f = lax.axis_index("feat")
    sibling = {"feat": 1 - f}
    greet([sibling])
    copy = remote(src, out.at[f], (send, recv), 0, sibling)
    copy.start()
    out[f] = src[...]
    copy.wait()


def fine_kernel(ranges, window, window_marks, small, large, out, keys, values_t, queries_t, scores):
    marks = window_marks[...]
    high = jnp.where((marks < 0) | (marks >= OUTSIDE), HI_ROWS - 1, marks // LO_ROWS)
    low = jnp.where(marks < 0, 0, marks % LO_ROWS)
    total = window.shape[1]
    count = out.shape[1]
    width = window.shape[0]
    heads = width // HEAD
    first = (total - count) // 2
    normed = norm(window[...]).astype(BF16)
    weight = [jnp.concatenate([small[0, i], small[1, i]], axis=0) for i in range(4)]
    queries_t[...] = dot(weight[0], normed[:, first:first + count]).astype(BF16)
    value_t = dot(weight[2], normed).astype(BF16)
    values_t[...] = jnp.concatenate([rows for h in range(heads) for rows in with_ones(value_t, h)], axis=0)
    key_t = dot(weight[1], normed).astype(BF16)

    def longest(rows):
        squares = jnp.square(rows.astype(F32))
        return jnp.max(jnp.sum(squares.reshape(heads, HEAD, rows.shape[1]), axis=1))

    small_scores = longest(queries_t[...]) * longest(key_t) * UNIT ** 2 <= BOUND ** 2
    for start in range(0, total, TILE):
        part = slice(start, start + TILE)
        hot_high = (lax.broadcasted_iota(jnp.int32, (HI_ROWS, TILE), 0) == high[:, part]).astype(F32)
        hot_low = (lax.broadcasted_iota(jnp.int32, (LO_ROWS, TILE), 0) == low[:, part]).astype(F32)
        key = key_t[:, part].astype(F32)
        stacked = jnp.concatenate([key, key, hot_high, hot_low], axis=0)
        keys[part, :] = jnp.transpose(stacked).astype(BF16)

    factor = jnp.where(small_scores, UNIT, HEAD ** (-0.5))

    def block(index, carry):
        columns = pl.ds(pl.multiple_of(index * TILE, TILE), TILE)
        middle = pl.ds(pl.multiple_of(first + index * TILE, TILE), TILE)
        own = window_marks[:, middle]
        hot_high = lax.broadcasted_iota(jnp.int32, (HI_ROWS, TILE), 0) == own // LO_ROWS
        hot_low = lax.broadcasted_iota(jnp.int32, (LO_ROWS, TILE), 0) == own % LO_ROWS
        barred = jnp.concatenate(
            [jnp.where(hot_high, 0.0, NEG_LARGE), jnp.where(hot_low, 0.0, NEG_LARGE)], axis=0
        ).astype(BF16)
        query = queries_t[:, columns]
        head_of = lax.broadcasted_iota(jnp.int32, (width, TILE), 0) // HEAD
        asked = jnp.concatenate(
            [jnp.concatenate(in_parts(query, head_of == h, factor) + [barred], axis=0) for h in range(heads)], axis=1
        )
        low_tile, high_tile = ranges[2 * index], ranges[2 * index + 1]

        def blend(tile, weights, sums):
            places = pl.ds(pl.multiple_of(tile * TILE, TILE), TILE)
            return tuple(
                sums[h]
                + dot(
                    values_t[h * VALUE_ROWS:(h + 1) * VALUE_ROWS, places],
                    weights[:, h * TILE:(h + 1) * TILE],
                )
                for h in range(heads)
            )

        def score(tile):
            return dot(keys[pl.ds(pl.multiple_of(tile * TILE, TILE), TILE), :], asked)

        nothing = tuple(jnp.zeros((VALUE_ROWS, TILE), F32) for _ in range(heads))

        def unshifted():
            def step(tile, sums):
                return blend(tile, jnp.exp2(score(tile)).astype(BF16), sums)

            return lax.fori_loop(low_tile, high_tile, step, nothing)

        def shifted():
            def rank(tile, top):
                got = score(tile)
                scores[pl.ds(pl.multiple_of((tile - low_tile) * TILE, TILE), TILE), :] = got
                return jnp.maximum(top, jnp.max(got.reshape(TILE // 8, 8, heads * TILE), axis=0))

            top = lax.fori_loop(low_tile, high_tile, rank, jnp.full((8, heads * TILE), -3e38, F32))
            top = jnp.max(top, axis=0, keepdims=True)

            def step(tile, sums):
                rows = pl.ds(pl.multiple_of((tile - low_tile) * TILE, TILE), TILE)
                return blend(tile, jnp.exp(scores[rows, :] - top).astype(BF16), sums)

            return lax.fori_loop(low_tile, high_tile, step, nothing)

        sums = lax.cond(small_scores, unshifted, shifted)
        mixed = jnp.concatenate([part[:HEAD] / part[HEAD:HEAD + 1] for part in sums], axis=0).astype(BF16)
        hidden = (window[:, middle].astype(F32) + dot(weight[3], mixed, TN)).astype(BF16)
        normed1 = norm(hidden).astype(BF16)
        fed = jnp.zeros((width, TILE), F32)
        for f in range(2):
            inner = gelu(dot(large[f, 0], normed1, TN)).astype(BF16)
            fed = fed + dot(large[f, 1], inner)
        out[:, columns] = (hidden.astype(F32) + fed).astype(BF16)
        return carry

    lax.fori_loop(0, count // TILE, block, 0)


def belongs(starts, ends, offset):
    places = lax.broadcasted_iota(jnp.int32, (TILE, SPAN), 0) + offset
    return jnp.where((places >= starts) & (places < ends), 1.0, 0.0).astype(BF16)


def pool_kernel(lows, fine, starts, ends, out, sums):
    sums[...] = jnp.zeros_like(sums)
    half = fine.shape[2]
    for index in range(2 * half // TILE):
        start = index * TILE
        near = pl.ds(pl.multiple_of(lows[index] * 128, 128), SPAN)
        owner = belongs(starts[:, near], ends[:, near], start)
        block = fine[start // half, :, start % half:start % half + TILE]
        sums[:, near] += dot(block, owner)
    rows = out.shape[1]
    mine = pl.ds(pl.multiple_of(lax.axis_index("feat") * rows, 128), rows)
    members = (ends[:, mine] - starts[:, mine]).astype(F32)
    out[...] = (sums[:, mine] / members).astype(BF16)


def coarse_kernel(serial_count, level_count, part, slots_all, own_slots, large, w_pool, w_up, out,
                  pooled, lifted, landed, keys, queries_t, values_t, nearby, send1, recv1, send2, recv2):
    s, l, f = lax.axis_index("serial"), lax.axis_index("level"), lax.axis_index("feat")
    other = 1 - f
    sibling = {"feat": other}
    peers = [{"serial": lax.rem(s + d, serial_count)} for d in range(1, serial_count)]
    origins = [lax.rem(s + serial_count - d, serial_count) for d in range(serial_count)]
    greet([sibling] + peers)
    count = part.shape[1]
    blocks = count // TILE

    def share(source, slot, send, recv, first):
        sems = (send, recv)
        copies = [remote(source, slot, sems, first, sibling)]
        copies += [remote(source, slot, sems, first + d, peer) for d, peer in enumerate(peers, 1)]
        for copy in copies[1:] + copies[:1]:
            copy.start()
        return copies

    def relay(slot, send, recv, index):
        copy = remote(slot, slot, (send, recv), index, sibling)
        copy.start()
        return copy

    copies = share(part, pooled.at[s, f], send1, recv1, 0)
    pooled[s, f] = part[...]
    base = ((s * level_count + l) * 2 + f) * count
    row = lax.broadcasted_iota(jnp.int32, (TILE, count), 0)
    landed[...] = jnp.zeros_like(landed)

    def land(origin, half):
        values = pooled[origin, half]
        columns = pl.ds(pl.multiple_of(half * count, TILE), count)
        wanted = slots_all[origin, :, columns] - base
        for index in range(blocks):
            chosen = jnp.where(wanted - index * TILE == row, 1.0, 0.0).astype(BF16)
            landed[:, index * TILE:(index + 1) * TILE] += dot(values, chosen, NT)

    land(s, f)
    copies[0].wait_recv()
    land(s, other)
    relays = []
    for d in range(1, serial_count):
        copies[d].wait_recv()
        relays.append(relay(pooled.at[origins[d], f], send1, recv1, serial_count + d - 1))
        land(origins[d], f)
        if d > 1:
            relays[d - 2].wait_recv()
            land(origins[d - 1], other)
    if relays:
        relays[-1].wait_recv()
        land(origins[-1], other)
    for copy in copies + relays:
        copy.wait_send()

    coarse = gelu(norm(dot(w_pool[...], landed[...].astype(BF16), TN))).astype(BF16)
    normed = norm(coarse).astype(BF16)
    weight = [jnp.concatenate([large[0, i], large[1, i]], axis=0) for i in range(2, 6)]
    width = coarse.shape[0]
    heads = width // HEAD
    queries_t[...] = (dot(weight[0], normed).astype(BF16) * HEAD ** (-0.5)).astype(BF16)
    value_t = dot(weight[2], normed).astype(BF16)
    values_t[...] = jnp.concatenate([rows for h in range(heads) for rows in with_ones(value_t, h)], axis=0)
    keys[...] = jnp.transpose(dot(weight[1], normed)).astype(BF16)
    head_of = lax.broadcasted_iota(jnp.int32, (width, TILE), 0) // HEAD
    stride = 2 * serial_count - 1
    sent, passed = [], []

    def forward(block):
        got = []
        for d in range(1, serial_count):
            sent[block][d].wait_recv()
            got.append(relay(lifted.at[origins[d], f, block], send2, recv2, block * stride + serial_count + d - 1))
        passed.append(got)

    for block in range(blocks):
        columns = slice(block * TILE, (block + 1) * TILE)
        query = queries_t[:, columns].astype(F32)
        parts = []
        for h in range(heads):
            got = dot(keys[...], jnp.where(head_of == h, query, 0.0).astype(BF16))
            weights = jnp.exp(got - jnp.max(got, axis=0, keepdims=True)).astype(BF16)
            sums = dot(values_t[h * VALUE_ROWS:(h + 1) * VALUE_ROWS, :], weights)
            parts.append(sums[:HEAD] / sums[HEAD:HEAD + 1])
        mixed = jnp.concatenate(parts, axis=0).astype(BF16)
        done = (coarse[:, columns].astype(F32) + dot(weight[3], mixed, TN)).astype(BF16)
        lifted[s, f, block] = dot(w_up[...], done).astype(BF16)
        slot = lifted.at[s, f, block]
        sent.append(share(slot, slot, send2, recv2, block * stride))
        if block > 0:
            forward(block - 1)

    nearby[...] = jnp.zeros_like(nearby)
    square = lax.broadcasted_iota(jnp.int32, (TILE, TILE), 0)

    def arrived(block):
        sent[block][0].wait_recv()
        for copy in passed[block]:
            copy.wait_recv()

    def fetch(chosen_blocks):
        def column(index, carry):
            columns = pl.ds(pl.multiple_of(index * TILE, TILE), TILE)
            wanted = own_slots[:, columns]
            total = nearby[:, columns]
            for origin in range(serial_count):
                for half in range(2):
                    start = ((origin * level_count + l) * 2 + half) * count
                    for block in chosen_blocks:
                        chosen = jnp.where(wanted - (start + block * TILE) == square, 1.0, 0.0).astype(BF16)
                        total = total + dot(lifted[origin, half, block], chosen)
            nearby[:, columns] = total
            return carry

        lax.fori_loop(0, own_slots.shape[1] // TILE, column, 0)

    for block in range(blocks - 2):
        arrived(block)
    fetch(range(blocks - 2))
    forward(blocks - 1)
    arrived(blocks - 2)
    fetch([blocks - 2])
    arrived(blocks - 1)
    fetch([blocks - 1])
    out[...] = nearby[...].astype(BF16)
    for group in sent + passed:
        for copy in group:
            copy.wait_send()


def spread_kernel(lows, nearby, fine, starts, ends, out):
    half = fine.shape[2]
    for index in range(2 * half // TILE):
        start = index * TILE
        near = pl.ds(pl.multiple_of(lows[index] * 128, 128), SPAN)
        owner = belongs(starts[:, near], ends[:, near], start)
        block = fine[start // half, :, start % half:start % half + TILE]
        out[:, start:start + TILE] = (block.astype(F32) + dot(nearby[:, near], owner, NT)).astype(BF16)


def call(kernel, outs, ins, scratch=(), collective=None):
    params = dict(vmem_limit_bytes=VMEM_BYTES)
    if collective is not None:
        params.update(collective_id=collective, has_side_effects=True)
    return pl.pallas_call(
        kernel,
        out_shape=[jax.ShapeDtypeStruct(shape, kind) for shape, kind in outs],
        in_specs=[SMEM if place == "scalar" else VMEM for place, _ in ins],
        out_specs=[VMEM] * len(outs),
        scratch_shapes=list(scratch),
        compiler_params=pltpu.CompilerParams(**params),
    )(*[value for _, value in ins])


def vectors(*values):
    return [("vector", value) for value in values]


def local(points, patch_ids, child_counts, voxel_slot, w_query0, w_key0, w_value0, w_attn_out0, w_mlp_in, w_mlp_out,
          w_pool, w_query1, w_key1, w_value1, w_attn_out1, w_up):
    rows, width = points.shape
    voxels = voxel_slot.shape[0]
    serial_count, level_count = lax.axis_size("serial"), lax.axis_size("level")
    dma = pltpu.SemaphoreType.DMA
    slots = voxel_slot.reshape(1, voxels)
    counts = child_counts.reshape(1, voxels)
    ends = jnp.cumsum(counts, axis=1)
    starts = ends - counts
    tiles = jnp.arange(rows // TILE, dtype=jnp.int32) * TILE
    lows = jnp.minimum(jnp.sum((ends <= tiles[:, None]).astype(jnp.int32), axis=1) // 128, (voxels - SPAN) // 128)

    window, window_marks, slots_all, small, large = call(
        functools.partial(prologue_kernel, serial_count, level_count),
        [
            ((width, rows), BF16), ((1, rows), jnp.int32), ((serial_count, 1, voxels), jnp.int32),
            ((2, 4) + w_query0.shape[::-1], BF16), ((2, 6) + w_mlp_in.shape, BF16),
        ],
        vectors(points.T, patch_ids.reshape(1, rows), slots, w_query0.T, w_key0.T, w_value0.T, w_attn_out0,
                w_mlp_in, w_mlp_out.T, w_query1.T, w_key1.T, w_value1.T, w_attn_out1),
        [dma((3 + serial_count,)), dma((3 + serial_count,)), dma((2,))],
        collective=0,
    )
    shard = lax.axis_index("serial") * level_count + lax.axis_index("level")
    f = lax.axis_index("feat")
    place = jnp.arange(rows, dtype=jnp.int32)[None, :]
    before = (shard == 0) & (f == 0) & (place < PATCH)
    after = (shard == serial_count * level_count - 1) & (f == 1) & (place >= rows - PATCH)
    window_marks = jnp.where(before, -1, jnp.where(after, OUTSIDE, window_marks))
    half = rows // 2
    asked = window_marks[0, half // 2:half // 2 + half].reshape(-1, TILE)
    low = jnp.sum((window_marks < asked[:, :1]).astype(jnp.int32), axis=1) // TILE
    high = (jnp.sum((window_marks <= asked[:, -1:]).astype(jnp.int32), axis=1) + TILE - 1) // TILE
    ranges = jnp.stack([low, high], axis=1).reshape(-1)

    (fine_half,) = call(
        fine_kernel,
        [((width, half), BF16)],
        [("scalar", ranges)] + vectors(window, window_marks, small, large),
        [
            pltpu.VMEM((rows, 2 * width + HI_ROWS + LO_ROWS), BF16), pltpu.VMEM((2 * width, rows), BF16),
            pltpu.VMEM((width, half), BF16), pltpu.VMEM((2 * PATCH + TILE, width // HEAD * TILE), F32),
        ],
    )
    (fine,) = call(swap_kernel, [((2, width, half), BF16)], vectors(fine_half), [dma((1,)), dma((1,))], collective=1)
    part = voxels // 2
    (pooled_part,) = call(
        pool_kernel,
        [((width, part), BF16)],
        [("scalar", lows)] + vectors(fine, starts, ends),
        [pltpu.VMEM((width, voxels), F32)],
    )

    wide = w_pool.shape[1]
    blocks = part // TILE
    each = 2 * serial_count - 1
    (nearby,) = call(
        functools.partial(coarse_kernel, serial_count, level_count),
        [((width, voxels), BF16)],
        vectors(pooled_part, slots_all, slots, large, w_pool, w_up.T),
        [
            pltpu.VMEM((serial_count, 2, width, part), BF16), pltpu.VMEM((serial_count, 2, blocks, width, TILE), BF16),
            pltpu.VMEM((width, part), F32), pltpu.VMEM((part, wide), BF16),
            pltpu.VMEM((wide, part), BF16), pltpu.VMEM((2 * wide, part), BF16), pltpu.VMEM((width, voxels), F32),
            dma((each,)), dma((each,)), dma((blocks * each,)), dma((blocks * each,)),
        ],
        collective=2,
    )
    (refined,) = call(
        spread_kernel,
        [((width, rows), BF16)],
        [("scalar", lows)] + vectors(nearby, fine, starts, ends),
    )
    return refined.T


def solution(mesh):
    shards = ("groups", "serial", "level")
    columns, stacked = P(None, "feat"), P("feat", None)
    in_specs = (
        P(shards, None), P(shards), P(shards, None), P(shards),
        columns, columns, columns, stacked, columns, stacked, P(),
        columns, columns, columns, stacked, P(),
    )
    return jax.shard_map(local, mesh=mesh, in_specs=in_specs, out_specs=P(shards, None), check_vma=False)
```

```python
import functools

import jax
import jax.numpy as jnp
from jax import lax
from jax.experimental import pallas as pl
from jax.experimental.pallas import tpu as pltpu
from jax.sharding import PartitionSpec as P

HEAD = 16
PATCH = 1024
EPSILON = 1e-05
NEG_LARGE = -1e30
TILE = 256
SPAN = 384
STACK = 2
HI_ROWS = 64
LO_ROWS = 128
OUTSIDE = 1 << 20
MESH = pl.DeviceIdType.MESH
BF16 = jnp.bfloat16
F32 = jnp.float32
VMEM = pl.BlockSpec(memory_space=pltpu.VMEM)
SMEM = pl.BlockSpec(memory_space=pltpu.SMEM)
VMEM_BYTES = 50 * 1024 * 1024

NN = (((1,), (0,)), ((), ()))
NT = (((1,), (1,)), ((), ()))
TN = (((0,), (0,)), ((), ()))


def dot(a, b, dims=NN):
    return lax.dot_general(a, b, dims, preferred_element_type=F32)


def norm(values):
    values = values.astype(F32)
    centre = values - jnp.mean(values, axis=0, keepdims=True)
    spread = jnp.mean(centre * centre, axis=0, keepdims=True)
    return centre * lax.rsqrt(spread + EPSILON)


def gelu(x):
    return 0.5 * x * (1.0 + jnp.tanh(0.7978845608028654 * (x + 0.044715 * (x * x * x))))


def greet(partners):
    barrier = pltpu.get_barrier_semaphore()
    for partner in partners:
        pl.semaphore_signal(barrier, inc=1, device_id=partner, device_id_type=MESH)
    pl.semaphore_wait(barrier, len(partners))


def remote(src, dst, sems, index, partner):
    send, recv = sems
    return pltpu.make_async_remote_copy(
        src_ref=src, dst_ref=dst, send_sem=send.at[index], recv_sem=recv.at[index],
        device_id=partner, device_id_type=MESH,
    )


def prologue_kernel(serial_count, level_count, points, marks, slots, q0, k0, v0, o0, m_in, m_out, q1, k1, v1, o1,
                    window, window_marks, slots_all, small, large, send, recv, local):
    s, l, f = lax.axis_index("serial"), lax.axis_index("level"), lax.axis_index("feat")
    other = 1 - f
    shard = s * level_count + l
    total = serial_count * level_count
    beside = lax.rem(shard + 2 * f - 1 + total, total)
    sibling = {"feat": other}
    edge = {"serial": beside // level_count, "level": lax.rem(beside, level_count), "feat": other}
    peers = [{"serial": lax.rem(s + d, serial_count)} for d in range(1, serial_count)]
    greet([sibling, edge] + peers)
    sems = (send, recv)
    rows = points.shape[1]
    kept = rows - PATCH
    src = pl.ds(pl.multiple_of(f * kept, PATCH), PATCH)
    dst = pl.ds(pl.multiple_of(other * kept, PATCH), PATCH)
    copies = [
        remote(points.at[:, src], window.at[:, dst], sems, 0, edge),
        remote(marks.at[:, src], window_marks.at[:, dst], sems, 1, edge),
    ]
    for copy in copies:
        copy.start()
    near = pl.ds(pl.multiple_of(f * PATCH, PATCH), kept)
    here = pl.ds(pl.multiple_of(other * PATCH, PATCH), kept)
    own = [
        pltpu.make_async_copy(points.at[:, near], window.at[:, here], local.at[0]),
        pltpu.make_async_copy(marks.at[:, near], window_marks.at[:, here], local.at[1]),
    ]
    for copy in own:
        copy.start()
    for place, part in enumerate((q0, k0, v0, o0)):
        small[f, place] = part[...]
    for place, part in enumerate((m_in, m_out, q1, k1, v1, o1)):
        large[f, place] = part[...]
    weights = [
        remote(small.at[f], small.at[f], sems, 2, sibling),
        remote(large.at[f], large.at[f], sems, 3, sibling),
    ]
    for copy in weights:
        copy.start()
    slots_all[s] = slots[...]
    for d, peer in enumerate(peers):
        copy = remote(slots, slots_all.at[s], sems, 4 + d, peer)
        copy.start()
        copies.append(copy)
    for copy in own + copies + weights:
        copy.wait()


def swap_kernel(src, out, send, recv):
    f = lax.axis_index("feat")
    sibling = {"feat": 1 - f}
    greet([sibling])
    copy = remote(src, out.at[f], (send, recv), 0, sibling)
    copy.start()
    out[f] = src[...]
    copy.wait()


def fine_kernel(ranges, window, window_marks, small, large, out, keys, values_t, queries_t, scores):
    marks = window_marks[...]
    high = jnp.where((marks < 0) | (marks >= OUTSIDE), HI_ROWS - 1, marks // LO_ROWS)
    low = jnp.where(marks < 0, 0, marks % LO_ROWS)
    total = window.shape[1]
    count = out.shape[1]
    width = window.shape[0]
    heads = width // HEAD
    first = (total - count) // 2
    normed = norm(window[...]).astype(BF16)
    weight = [jnp.concatenate([small[0, i], small[1, i]], axis=0) for i in range(4)]
    queries_t[...] = (dot(weight[0], normed[:, first:first + count]).astype(BF16) * HEAD ** (-0.5)).astype(BF16)
    values_t[...] = dot(weight[2], normed).astype(BF16)
    key_t = dot(weight[1], normed).astype(BF16)
    for start in range(0, total, TILE):
        part = slice(start, start + TILE)
        hot_high = (lax.broadcasted_iota(jnp.int32, (HI_ROWS, TILE), 0) == high[:, part]).astype(F32)
        hot_low = (lax.broadcasted_iota(jnp.int32, (LO_ROWS, TILE), 0) == low[:, part]).astype(F32)
        stacked = jnp.concatenate([key_t[:, part].astype(F32), hot_high, hot_low], axis=0)
        keys[part, :] = jnp.transpose(stacked).astype(BF16)

    def block(index, carry):
        columns = pl.ds(pl.multiple_of(index * TILE, TILE), TILE)
        middle = pl.ds(pl.multiple_of(first + index * TILE, TILE), TILE)
        own = window_marks[:, middle]
        hot_high = lax.broadcasted_iota(jnp.int32, (HI_ROWS, TILE), 0) == own // LO_ROWS
        hot_low = lax.broadcasted_iota(jnp.int32, (LO_ROWS, TILE), 0) == own % LO_ROWS
        barred = jnp.concatenate(
            [jnp.where(hot_high, 0.0, NEG_LARGE), jnp.where(hot_low, 0.0, NEG_LARGE)], axis=0
        ).astype(BF16)
        query = queries_t[:, columns].astype(F32)
        head_of = lax.broadcasted_iota(jnp.int32, (width, TILE), 0) // HEAD
        asked = jnp.concatenate(
            [
                jnp.concatenate([jnp.where(head_of == h, query, 0.0).astype(BF16), barred], axis=0)
                for h in range(heads)
            ],
            axis=1,
        )
        low_tile, high_tile = ranges[2 * index], ranges[2 * index + 1]

        def score(tile, top):
            rows = pl.ds(pl.multiple_of(tile * TILE, TILE), TILE)
            got = dot(keys[rows, :], asked)
            scores[pl.ds(pl.multiple_of((tile - low_tile) * TILE, TILE), TILE), :] = got
            return jnp.maximum(top, jnp.max(got.reshape(TILE // 8, 8, heads * TILE), axis=0))

        top = lax.fori_loop(low_tile, high_tile, score, jnp.full((8, heads * TILE), -3e38, F32))
        top = jnp.max(top, axis=0, keepdims=True)

        def mix(tile, state):
            total_weight, sums = state
            rows = pl.ds(pl.multiple_of((tile - low_tile) * TILE, TILE), TILE)
            places = pl.ds(pl.multiple_of(tile * TILE, TILE), TILE)
            weights = jnp.exp(scores[rows, :] - top)
            total_weight = total_weight + jnp.sum(weights.reshape(TILE // 8, 8, heads * TILE), axis=0)
            rounded = weights.astype(BF16)
            sums = tuple(
                sums[h]
                + dot(values_t[h * HEAD:(h + 1) * HEAD, places], rounded[:, h * TILE:(h + 1) * TILE])
                for h in range(heads)
            )
            return total_weight, sums

        total_weight, sums = lax.fori_loop(
            low_tile, high_tile, mix,
            (jnp.zeros((8, heads * TILE), F32), tuple(jnp.zeros((HEAD, TILE), F32) for _ in range(heads))),
        )
        total_weight = jnp.sum(total_weight, axis=0, keepdims=True)
        mixed = jnp.concatenate(
            [sums[h] / total_weight[:, h * TILE:(h + 1) * TILE] for h in range(heads)], axis=0
        ).astype(BF16)
        hidden = (window[:, middle].astype(F32) + dot(weight[3], mixed, TN)).astype(BF16)
        normed1 = norm(hidden).astype(BF16)
        fed = jnp.zeros((width, TILE), F32)
        for f in range(2):
            inner = gelu(dot(large[f, 0], normed1, TN)).astype(BF16)
            fed = fed + dot(large[f, 1], inner)
        out[:, columns] = (hidden.astype(F32) + fed).astype(BF16)
        return carry

    lax.fori_loop(0, count // TILE, block, 0)


def belongs(starts, ends, offset):
    places = lax.broadcasted_iota(jnp.int32, (TILE, SPAN), 0) + offset
    return jnp.where((places >= starts) & (places < ends), 1.0, 0.0).astype(BF16)


def pool_kernel(lows, fine, starts, ends, out, sums):
    sums[...] = jnp.zeros_like(sums)
    half = fine.shape[2]
    for index in range(2 * half // TILE):
        start = index * TILE
        near = pl.ds(pl.multiple_of(lows[index] * 128, 128), SPAN)
        owner = belongs(starts[:, near], ends[:, near], start)
        block = fine[start // half, :, start % half:start % half + TILE]
        sums[:, near] += dot(block, owner)
    rows = out.shape[1]
    mine = pl.ds(pl.multiple_of(lax.axis_index("feat") * rows, 128), rows)
    members = (ends[:, mine] - starts[:, mine]).astype(F32)
    out[...] = (sums[:, mine] / members).astype(BF16)


def coarse_kernel(serial_count, level_count, part, slots_all, own_slots, large, w_pool, w_up, out,
                  pooled, lifted, landed, keys_t, queries, values, nearby, send1, recv1, send2, recv2):
    s, l, f = lax.axis_index("serial"), lax.axis_index("level"), lax.axis_index("feat")
    other = 1 - f
    sibling = {"feat": other}
    peers = [{"serial": lax.rem(s + d, serial_count)} for d in range(1, serial_count)]
    origins = [lax.rem(s + serial_count - d, serial_count) for d in range(serial_count)]
    greet([sibling] + peers)
    count = part.shape[1]
    blocks = count // TILE

    def share(source, slot, send, recv, first):
        sems = (send, recv)
        copies = [remote(source, slot, sems, first, sibling)]
        copies += [remote(source, slot, sems, first + d, peer) for d, peer in enumerate(peers, 1)]
        for copy in copies[1:] + copies[:1]:
            copy.start()
        return copies

    def relay(slot, send, recv, index):
        copy = remote(slot, slot, (send, recv), index, sibling)
        copy.start()
        return copy

    copies = share(part, pooled.at[s, f], send1, recv1, 0)
    pooled[s, f] = part[...]
    base = ((s * level_count + l) * 2 + f) * count
    row = lax.broadcasted_iota(jnp.int32, (TILE, count), 0)
    landed[...] = jnp.zeros_like(landed)

    def land(origin, half):
        values = pooled[origin, half]
        columns = pl.ds(pl.multiple_of(half * count, TILE), count)
        wanted = slots_all[origin, :, columns] - base
        for index in range(blocks):
            chosen = jnp.where(wanted - index * TILE == row, 1.0, 0.0).astype(BF16)
            landed[:, index * TILE:(index + 1) * TILE] += dot(values, chosen, NT)

    land(s, f)
    copies[0].wait_recv()
    land(s, other)
    relays = []
    for d in range(1, serial_count):
        copies[d].wait_recv()
        relays.append(relay(pooled.at[origins[d], f], send1, recv1, serial_count + d - 1))
        land(origins[d], f)
        if d > 1:
            relays[d - 2].wait_recv()
            land(origins[d - 1], other)
    if relays:
        relays[-1].wait_recv()
        land(origins[-1], other)
    for copy in copies + relays:
        copy.wait_send()

    coarse = gelu(norm(dot(w_pool[...], landed[...].astype(BF16), TN))).astype(BF16)
    normed = norm(coarse).astype(BF16)
    weight = [jnp.concatenate([large[0, i], large[1, i]], axis=0) for i in range(2, 6)]
    width = coarse.shape[0]
    heads = width // HEAD
    normed_rows = jnp.transpose(normed.astype(F32)).astype(BF16)
    queries[...] = (dot(normed_rows, weight[0], NT).astype(BF16) * HEAD ** (-0.5)).astype(BF16)
    values[...] = dot(normed_rows, weight[2], NT).astype(BF16)
    keys_t[...] = dot(weight[1], normed).astype(BF16)
    head_of = lax.broadcasted_iota(jnp.int32, (TILE, width), 1) // HEAD
    stride = 2 * serial_count - 1
    sent, passed = [], []

    def forward(block):
        got = []
        for d in range(1, serial_count):
            sent[block][d].wait_recv()
            got.append(relay(lifted.at[origins[d], f, block], send2, recv2, block * stride + serial_count + d - 1))
        passed.append(got)

    for block in range(blocks):
        columns = slice(block * TILE, (block + 1) * TILE)
        query = queries[columns, :].astype(F32)
        mixed = jnp.zeros((TILE, width), F32)
        for first in range(0, heads, STACK):
            asked = jnp.concatenate(
                [jnp.where(head_of == first + i, query, 0.0).astype(BF16) for i in range(STACK)], axis=0
            )
            got = dot(asked, keys_t[...])
            weights = jnp.exp(got - jnp.max(got, axis=1, keepdims=True))
            sums = dot(weights.astype(BF16), values[...]) / jnp.sum(weights, axis=1, keepdims=True)
            for i in range(STACK):
                mixed = jnp.where(head_of == first + i, sums[i * TILE:(i + 1) * TILE], mixed)
        mixed = jnp.transpose(mixed).astype(BF16)
        done = (coarse[:, columns].astype(F32) + dot(weight[3], mixed, TN)).astype(BF16)
        lifted[s, f, block] = dot(w_up[...], done).astype(BF16)
        slot = lifted.at[s, f, block]
        sent.append(share(slot, slot, send2, recv2, block * stride))
        if block > 0:
            forward(block - 1)

    nearby[...] = jnp.zeros_like(nearby)
    square = lax.broadcasted_iota(jnp.int32, (TILE, TILE), 0)

    def arrived(block):
        sent[block][0].wait_recv()
        for copy in passed[block]:
            copy.wait_recv()

    def fetch(chosen_blocks):
        def column(index, carry):
            columns = pl.ds(pl.multiple_of(index * TILE, TILE), TILE)
            wanted = own_slots[:, columns]
            total = nearby[:, columns]
            for origin in range(serial_count):
                for half in range(2):
                    start = ((origin * level_count + l) * 2 + half) * count
                    for block in chosen_blocks:
                        chosen = jnp.where(wanted - (start + block * TILE) == square, 1.0, 0.0).astype(BF16)
                        total = total + dot(lifted[origin, half, block], chosen)
            nearby[:, columns] = total
            return carry

        lax.fori_loop(0, own_slots.shape[1] // TILE, column, 0)

    for block in range(blocks - 2):
        arrived(block)
    fetch(range(blocks - 2))
    forward(blocks - 1)
    arrived(blocks - 2)
    fetch([blocks - 2])
    arrived(blocks - 1)
    fetch([blocks - 1])
    out[...] = nearby[...].astype(BF16)
    for group in sent + passed:
        for copy in group:
            copy.wait_send()


def spread_kernel(lows, nearby, fine, starts, ends, out):
    half = fine.shape[2]
    for index in range(2 * half // TILE):
        start = index * TILE
        near = pl.ds(pl.multiple_of(lows[index] * 128, 128), SPAN)
        owner = belongs(starts[:, near], ends[:, near], start)
        block = fine[start // half, :, start % half:start % half + TILE]
        out[:, start:start + TILE] = (block.astype(F32) + dot(nearby[:, near], owner, NT)).astype(BF16)


def call(kernel, outs, ins, scratch=(), collective=None):
    params = dict(vmem_limit_bytes=VMEM_BYTES)
    if collective is not None:
        params.update(collective_id=collective, has_side_effects=True)
    return pl.pallas_call(
        kernel,
        out_shape=[jax.ShapeDtypeStruct(shape, kind) for shape, kind in outs],
        in_specs=[SMEM if place == "scalar" else VMEM for place, _ in ins],
        out_specs=[VMEM] * len(outs),
        scratch_shapes=list(scratch),
        compiler_params=pltpu.CompilerParams(**params),
    )(*[value for _, value in ins])


def vectors(*values):
    return [("vector", value) for value in values]


def local(points, patch_ids, child_counts, voxel_slot, w_query0, w_key0, w_value0, w_attn_out0, w_mlp_in, w_mlp_out,
          w_pool, w_query1, w_key1, w_value1, w_attn_out1, w_up):
    rows, width = points.shape
    voxels = voxel_slot.shape[0]
    serial_count, level_count = lax.axis_size("serial"), lax.axis_size("level")
    dma = pltpu.SemaphoreType.DMA
    slots = voxel_slot.reshape(1, voxels)
    counts = child_counts.reshape(1, voxels)
    ends = jnp.cumsum(counts, axis=1)
    starts = ends - counts
    tiles = jnp.arange(rows // TILE, dtype=jnp.int32) * TILE
    lows = jnp.minimum(jnp.sum((ends <= tiles[:, None]).astype(jnp.int32), axis=1) // 128, (voxels - SPAN) // 128)

    window, window_marks, slots_all, small, large = call(
        functools.partial(prologue_kernel, serial_count, level_count),
        [
            ((width, rows), BF16), ((1, rows), jnp.int32), ((serial_count, 1, voxels), jnp.int32),
            ((2, 4) + w_query0.shape[::-1], BF16), ((2, 6) + w_mlp_in.shape, BF16),
        ],
        vectors(points.T, patch_ids.reshape(1, rows), slots, w_query0.T, w_key0.T, w_value0.T, w_attn_out0,
                w_mlp_in, w_mlp_out.T, w_query1.T, w_key1.T, w_value1.T, w_attn_out1),
        [dma((3 + serial_count,)), dma((3 + serial_count,)), dma((2,))],
        collective=0,
    )
    shard = lax.axis_index("serial") * level_count + lax.axis_index("level")
    f = lax.axis_index("feat")
    place = jnp.arange(rows, dtype=jnp.int32)[None, :]
    before = (shard == 0) & (f == 0) & (place < PATCH)
    after = (shard == serial_count * level_count - 1) & (f == 1) & (place >= rows - PATCH)
    window_marks = jnp.where(before, -1, jnp.where(after, OUTSIDE, window_marks))
    half = rows // 2
    asked = window_marks[0, half // 2:half // 2 + half].reshape(-1, TILE)
    low = jnp.sum((window_marks < asked[:, :1]).astype(jnp.int32), axis=1) // TILE
    high = (jnp.sum((window_marks <= asked[:, -1:]).astype(jnp.int32), axis=1) + TILE - 1) // TILE
    ranges = jnp.stack([low, high], axis=1).reshape(-1)

    (fine_half,) = call(
        fine_kernel,
        [((width, half), BF16)],
        [("scalar", ranges)] + vectors(window, window_marks, small, large),
        [
            pltpu.VMEM((rows, width + HI_ROWS + LO_ROWS), BF16), pltpu.VMEM((width, rows), BF16),
            pltpu.VMEM((width, half), BF16), pltpu.VMEM((2 * PATCH + TILE, width // HEAD * TILE), F32),
        ],
    )
    (fine,) = call(swap_kernel, [((2, width, half), BF16)], vectors(fine_half), [dma((1,)), dma((1,))], collective=1)
    part = voxels // 2
    (pooled_part,) = call(
        pool_kernel,
        [((width, part), BF16)],
        [("scalar", lows)] + vectors(fine, starts, ends),
        [pltpu.VMEM((width, voxels), F32)],
    )

    wide = w_pool.shape[1]
    blocks = part // TILE
    each = 2 * serial_count - 1
    (nearby,) = call(
        functools.partial(coarse_kernel, serial_count, level_count),
        [((width, voxels), BF16)],
        vectors(pooled_part, slots_all, slots, large, w_pool, w_up.T),
        [
            pltpu.VMEM((serial_count, 2, width, part), BF16), pltpu.VMEM((serial_count, 2, blocks, width, TILE), BF16),
            pltpu.VMEM((width, part), F32), pltpu.VMEM((wide, part), BF16),
            pltpu.VMEM((part, wide), BF16), pltpu.VMEM((part, wide), BF16), pltpu.VMEM((width, voxels), F32),
            dma((each,)), dma((each,)), dma((blocks * each,)), dma((blocks * each,)),
        ],
        collective=2,
    )
    (refined,) = call(
        spread_kernel,
        [((width, rows), BF16)],
        [("scalar", lows)] + vectors(nearby, fine, starts, ends),
    )
    return refined.T


def solution(mesh):
    shards = ("groups", "serial", "level")
    columns, stacked = P(None, "feat"), P("feat", None)
    in_specs = (
        P(shards, None), P(shards), P(shards, None), P(shards),
        columns, columns, columns, stacked, columns, stacked, P(),
        columns, columns, columns, stacked, P(),
    )
    return jax.shard_map(local, mesh=mesh, in_specs=in_specs, out_specs=P(shards, None), check_vma=False)
```

```python
import functools

import jax
import jax.numpy as jnp
from jax import lax
from jax.experimental import pallas as pl
from jax.experimental.pallas import tpu as pltpu
from jax.sharding import PartitionSpec as P

HEAD = 16
PATCH = 1024
EPSILON = 1e-05
NEG_LARGE = -1e30
TILE = 256
SPAN = 384
STACK = 2
HI_ROWS = 32
LO_ROWS = 32
OUTSIDE = 1 << 20
MESH = pl.DeviceIdType.MESH
BF16 = jnp.bfloat16
F32 = jnp.float32
VMEM = pl.BlockSpec(memory_space=pltpu.VMEM)
SMEM = pl.BlockSpec(memory_space=pltpu.SMEM)
VMEM_BYTES = 50 * 1024 * 1024

NN = (((1,), (0,)), ((), ()))
NT = (((1,), (1,)), ((), ()))
TN = (((0,), (0,)), ((), ()))


def dot(a, b, dims=NN):
    return lax.dot_general(a, b, dims, preferred_element_type=F32)


def norm(values):
    values = values.astype(F32)
    centre = values - jnp.mean(values, axis=0, keepdims=True)
    spread = jnp.mean(centre * centre, axis=0, keepdims=True)
    return centre * lax.rsqrt(spread + EPSILON)


def gelu(x):
    return 0.5 * x * (1.0 + jnp.tanh(0.7978845608028654 * (x + 0.044715 * (x * x * x))))


def greet(partners):
    barrier = pltpu.get_barrier_semaphore()
    for partner in partners:
        pl.semaphore_signal(barrier, inc=1, device_id=partner, device_id_type=MESH)
    pl.semaphore_wait(barrier, len(partners))


def remote(src, dst, sems, index, partner):
    send, recv = sems
    return pltpu.make_async_remote_copy(
        src_ref=src, dst_ref=dst, send_sem=send.at[index], recv_sem=recv.at[index],
        device_id=partner, device_id_type=MESH,
    )


def prologue_kernel(serial_count, level_count, points, marks, slots, q0, k0, v0, o0, m_in, m_out, q1, k1, v1, o1,
                    window, window_marks, slots_all, small, large, send, recv, local):
    s, l, f = lax.axis_index("serial"), lax.axis_index("level"), lax.axis_index("feat")
    other = 1 - f
    shard = s * level_count + l
    total = serial_count * level_count
    beside = lax.rem(shard + 2 * f - 1 + total, total)
    sibling = {"feat": other}
    edge = {"serial": beside // level_count, "level": lax.rem(beside, level_count), "feat": other}
    peers = [{"serial": lax.rem(s + d, serial_count)} for d in range(1, serial_count)]
    greet([sibling, edge] + peers)
    sems = (send, recv)
    rows = points.shape[1]
    kept = rows - PATCH
    src = pl.ds(pl.multiple_of(f * kept, PATCH), PATCH)
    dst = pl.ds(pl.multiple_of(other * kept, PATCH), PATCH)
    copies = [
        remote(points.at[:, src], window.at[:, dst], sems, 0, edge),
        remote(marks.at[:, src], window_marks.at[:, dst], sems, 1, edge),
    ]
    for copy in copies:
        copy.start()
    near = pl.ds(pl.multiple_of(f * PATCH, PATCH), kept)
    here = pl.ds(pl.multiple_of(other * PATCH, PATCH), kept)
    own = [
        pltpu.make_async_copy(points.at[:, near], window.at[:, here], local.at[0]),
        pltpu.make_async_copy(marks.at[:, near], window_marks.at[:, here], local.at[1]),
    ]
    for copy in own:
        copy.start()
    for place, part in enumerate((q0, k0, v0, o0)):
        small[f, place] = part[...]
    for place, part in enumerate((m_in, m_out, q1, k1, v1, o1)):
        large[f, place] = part[...]
    weights = [
        remote(small.at[f], small.at[f], sems, 2, sibling),
        remote(large.at[f], large.at[f], sems, 3, sibling),
    ]
    for copy in weights:
        copy.start()
    slots_all[s] = slots[...]
    for d, peer in enumerate(peers):
        copy = remote(slots, slots_all.at[s], sems, 4 + d, peer)
        copy.start()
        copies.append(copy)
    for copy in own + copies + weights:
        copy.wait()


def swap_kernel(src, out, send, recv):
    f = lax.axis_index("feat")
    sibling = {"feat": 1 - f}
    greet([sibling])
    copy = remote(src, out.at[f], (send, recv), 0, sibling)
    copy.start()
    out[f] = src[...]
    copy.wait()


def fine_kernel(ranges, window, window_marks, small, large, out, keys, values_t, queries_t, scores):
    marks = window_marks[...]
    outside = jnp.where((marks < 0) | (marks >= OUTSIDE), 1, 0)
    high = marks // LO_ROWS
    low = marks % LO_ROWS
    total = window.shape[1]
    count = out.shape[1]
    width = window.shape[0]
    heads = width // HEAD
    first = (total - count) // 2
    normed = norm(window[...]).astype(BF16)
    weight = [jnp.concatenate([small[0, i], small[1, i]], axis=0) for i in range(4)]
    queries_t[...] = (dot(weight[0], normed[:, first:first + count]).astype(BF16) * HEAD ** (-0.5)).astype(BF16)
    values_t[...] = dot(weight[2], normed).astype(BF16)
    key_t = dot(weight[1], normed).astype(BF16)
    for start in range(0, total, TILE):
        part = slice(start, start + TILE)
        code = lax.broadcasted_iota(jnp.int32, (HI_ROWS, TILE), 0)
        hot_high = ((code == high[:, part]) | (outside[:, part] > 0)).astype(F32)
        hot_low = (lax.broadcasted_iota(jnp.int32, (LO_ROWS, TILE), 0) == low[:, part]).astype(F32)
        stacked = jnp.concatenate([key_t[:, part].astype(F32), hot_high, hot_low], axis=0)
        keys[part, :] = jnp.transpose(stacked).astype(BF16)

    def block(index, carry):
        columns = pl.ds(pl.multiple_of(index * TILE, TILE), TILE)
        middle = pl.ds(pl.multiple_of(first + index * TILE, TILE), TILE)
        own = window_marks[:, middle]
        hot_high = lax.broadcasted_iota(jnp.int32, (HI_ROWS, TILE), 0) == own // LO_ROWS
        hot_low = lax.broadcasted_iota(jnp.int32, (LO_ROWS, TILE), 0) == own % LO_ROWS
        barred = jnp.concatenate(
            [jnp.where(hot_high, 0.0, NEG_LARGE), jnp.where(hot_low, 0.0, NEG_LARGE)], axis=0
        ).astype(BF16)
        query = queries_t[:, columns].astype(F32)
        head_of = lax.broadcasted_iota(jnp.int32, (width, TILE), 0) // HEAD
        asked = jnp.concatenate(
            [
                jnp.concatenate([jnp.where(head_of == h, query, 0.0).astype(BF16), barred], axis=0)
                for h in range(heads)
            ],
            axis=1,
        )
        low_tile, high_tile = ranges[2 * index], ranges[2 * index + 1]

        def score(tile, top):
            rows = pl.ds(pl.multiple_of(tile * TILE, TILE), TILE)
            got = dot(keys[rows, :], asked)
            scores[pl.ds(pl.multiple_of((tile - low_tile) * TILE, TILE), TILE), :] = got
            return jnp.maximum(top, jnp.max(got.reshape(TILE // 8, 8, heads * TILE), axis=0))

        top = lax.fori_loop(low_tile, high_tile, score, jnp.full((8, heads * TILE), -3e38, F32))
        top = jnp.max(top, axis=0, keepdims=True)

        def mix(tile, state):
            total_weight, sums = state
            rows = pl.ds(pl.multiple_of((tile - low_tile) * TILE, TILE), TILE)
            places = pl.ds(pl.multiple_of(tile * TILE, TILE), TILE)
            weights = jnp.exp(scores[rows, :] - top)
            total_weight = total_weight + jnp.sum(weights.reshape(TILE // 8, 8, heads * TILE), axis=0)
            rounded = weights.astype(BF16)
            sums = tuple(
                sums[h]
                + dot(values_t[h * HEAD:(h + 1) * HEAD, places], rounded[:, h * TILE:(h + 1) * TILE])
                for h in range(heads)
            )
            return total_weight, sums

        total_weight, sums = lax.fori_loop(
            low_tile, high_tile, mix,
            (jnp.zeros((8, heads * TILE), F32), tuple(jnp.zeros((HEAD, TILE), F32) for _ in range(heads))),
        )
        total_weight = jnp.sum(total_weight, axis=0, keepdims=True)
        mixed = jnp.concatenate(
            [sums[h] / total_weight[:, h * TILE:(h + 1) * TILE] for h in range(heads)], axis=0
        ).astype(BF16)
        hidden = (window[:, middle].astype(F32) + dot(weight[3], mixed, TN)).astype(BF16)
        normed1 = norm(hidden).astype(BF16)
        fed = jnp.zeros((width, TILE), F32)
        for f in range(2):
            inner = gelu(dot(large[f, 0], normed1, TN)).astype(BF16)
            fed = fed + dot(large[f, 1], inner)
        out[:, columns] = (hidden.astype(F32) + fed).astype(BF16)
        return carry

    lax.fori_loop(0, count // TILE, block, 0)


def belongs(starts, ends, offset):
    places = lax.broadcasted_iota(jnp.int32, (TILE, SPAN), 0) + offset
    return jnp.where((places >= starts) & (places < ends), 1.0, 0.0).astype(BF16)


def pool_kernel(lows, fine, starts, ends, out, sums):
    sums[...] = jnp.zeros_like(sums)
    half = fine.shape[2]
    for index in range(2 * half // TILE):
        start = index * TILE
        near = pl.ds(pl.multiple_of(lows[index] * 128, 128), SPAN)
        owner = belongs(starts[:, near], ends[:, near], start)
        block = fine[start // half, :, start % half:start % half + TILE]
        sums[:, near] += dot(block, owner)
    rows = out.shape[1]
    mine = pl.ds(pl.multiple_of(lax.axis_index("feat") * rows, 128), rows)
    members = (ends[:, mine] - starts[:, mine]).astype(F32)
    out[...] = (sums[:, mine] / members).astype(BF16)


def coarse_kernel(serial_count, level_count, part, slots_all, own_slots, large, w_pool, w_up, out,
                  pooled, lifted, landed, keys_t, queries, values, nearby, send1, recv1, send2, recv2):
    s, l, f = lax.axis_index("serial"), lax.axis_index("level"), lax.axis_index("feat")
    other = 1 - f
    sibling = {"feat": other}
    peers = [{"serial": lax.rem(s + d, serial_count)} for d in range(1, serial_count)]
    origins = [lax.rem(s + serial_count - d, serial_count) for d in range(serial_count)]
    greet([sibling] + peers)
    count = part.shape[1]
    blocks = count // TILE

    def share(source, slot, send, recv, first):
        sems = (send, recv)
        copies = [remote(source, slot, sems, first, sibling)]
        copies += [remote(source, slot, sems, first + d, peer) for d, peer in enumerate(peers, 1)]
        for copy in copies[1:] + copies[:1]:
            copy.start()
        return copies

    def relay(slot, send, recv, index):
        copy = remote(slot, slot, (send, recv), index, sibling)
        copy.start()
        return copy

    copies = share(part, pooled.at[s, f], send1, recv1, 0)
    pooled[s, f] = part[...]
    base = ((s * level_count + l) * 2 + f) * count
    row = lax.broadcasted_iota(jnp.int32, (TILE, count), 0)
    landed[...] = jnp.zeros_like(landed)

    def land(origin, half):
        values = pooled[origin, half]
        columns = pl.ds(pl.multiple_of(half * count, TILE), count)
        wanted = slots_all[origin, :, columns] - base
        for index in range(blocks):
            chosen = jnp.where(wanted - index * TILE == row, 1.0, 0.0).astype(BF16)
            landed[:, index * TILE:(index + 1) * TILE] += dot(values, chosen, NT)

    land(s, f)
    copies[0].wait_recv()
    land(s, other)
    relays = []
    for d in range(1, serial_count):
        copies[d].wait_recv()
        relays.append(relay(pooled.at[origins[d], f], send1, recv1, serial_count + d - 1))
        land(origins[d], f)
        if d > 1:
            relays[d - 2].wait_recv()
            land(origins[d - 1], other)
    if relays:
        relays[-1].wait_recv()
        land(origins[-1], other)
    for copy in copies + relays:
        copy.wait_send()

    coarse = gelu(norm(dot(w_pool[...], landed[...].astype(BF16), TN))).astype(BF16)
    normed = norm(coarse).astype(BF16)
    weight = [jnp.concatenate([large[0, i], large[1, i]], axis=0) for i in range(2, 6)]
    width = coarse.shape[0]
    heads = width // HEAD
    normed_rows = jnp.transpose(normed.astype(F32)).astype(BF16)
    queries[...] = (dot(normed_rows, weight[0], NT).astype(BF16) * HEAD ** (-0.5)).astype(BF16)
    values[...] = dot(normed_rows, weight[2], NT).astype(BF16)
    keys_t[...] = dot(weight[1], normed).astype(BF16)
    head_of = lax.broadcasted_iota(jnp.int32, (TILE, width), 1) // HEAD
    stride = 2 * serial_count - 1
    sent, passed = [], []

    def forward(block):
        got = []
        for d in range(1, serial_count):
            sent[block][d].wait_recv()
            got.append(relay(lifted.at[origins[d], f, block], send2, recv2, block * stride + serial_count + d - 1))
        passed.append(got)

    for block in range(blocks):
        columns = slice(block * TILE, (block + 1) * TILE)
        query = queries[columns, :].astype(F32)
        mixed = jnp.zeros((TILE, width), F32)
        for first in range(0, heads, STACK):
            asked = jnp.concatenate(
                [jnp.where(head_of == first + i, query, 0.0).astype(BF16) for i in range(STACK)], axis=0
            )
            got = dot(asked, keys_t[...])
            weights = jnp.exp(got - jnp.max(got, axis=1, keepdims=True))
            sums = dot(weights.astype(BF16), values[...]) / jnp.sum(weights, axis=1, keepdims=True)
            for i in range(STACK):
                mixed = jnp.where(head_of == first + i, sums[i * TILE:(i + 1) * TILE], mixed)
        mixed = jnp.transpose(mixed).astype(BF16)
        done = (coarse[:, columns].astype(F32) + dot(weight[3], mixed, TN)).astype(BF16)
        lifted[s, f, block] = dot(w_up[...], done).astype(BF16)
        slot = lifted.at[s, f, block]
        sent.append(share(slot, slot, send2, recv2, block * stride))
        if block > 0:
            forward(block - 1)

    nearby[...] = jnp.zeros_like(nearby)
    square = lax.broadcasted_iota(jnp.int32, (TILE, TILE), 0)

    def arrived(block):
        sent[block][0].wait_recv()
        for copy in passed[block]:
            copy.wait_recv()

    def fetch(chosen_blocks):
        def column(index, carry):
            columns = pl.ds(pl.multiple_of(index * TILE, TILE), TILE)
            wanted = own_slots[:, columns]
            total = nearby[:, columns]
            for origin in range(serial_count):
                for half in range(2):
                    start = ((origin * level_count + l) * 2 + half) * count
                    for block in chosen_blocks:
                        chosen = jnp.where(wanted - (start + block * TILE) == square, 1.0, 0.0).astype(BF16)
                        total = total + dot(lifted[origin, half, block], chosen)
            nearby[:, columns] = total
            return carry

        lax.fori_loop(0, own_slots.shape[1] // TILE, column, 0)

    for block in range(blocks - 2):
        arrived(block)
    fetch(range(blocks - 2))
    forward(blocks - 1)
    arrived(blocks - 2)
    fetch([blocks - 2])
    arrived(blocks - 1)
    fetch([blocks - 1])
    out[...] = nearby[...].astype(BF16)
    for group in sent + passed:
        for copy in group:
            copy.wait_send()


def spread_kernel(lows, nearby, fine, starts, ends, out):
    half = fine.shape[2]
    for index in range(2 * half // TILE):
        start = index * TILE
        near = pl.ds(pl.multiple_of(lows[index] * 128, 128), SPAN)
        owner = belongs(starts[:, near], ends[:, near], start)
        block = fine[start // half, :, start % half:start % half + TILE]
        out[:, start:start + TILE] = (block.astype(F32) + dot(nearby[:, near], owner, NT)).astype(BF16)


def call(kernel, outs, ins, scratch=(), collective=None):
    params = dict(vmem_limit_bytes=VMEM_BYTES)
    if collective is not None:
        params.update(collective_id=collective, has_side_effects=True)
    return pl.pallas_call(
        kernel,
        out_shape=[jax.ShapeDtypeStruct(shape, kind) for shape, kind in outs],
        in_specs=[SMEM if place == "scalar" else VMEM for place, _ in ins],
        out_specs=[VMEM] * len(outs),
        scratch_shapes=list(scratch),
        compiler_params=pltpu.CompilerParams(**params),
    )(*[value for _, value in ins])


def vectors(*values):
    return [("vector", value) for value in values]


def local(points, patch_ids, child_counts, voxel_slot, w_query0, w_key0, w_value0, w_attn_out0, w_mlp_in, w_mlp_out,
          w_pool, w_query1, w_key1, w_value1, w_attn_out1, w_up):
    rows, width = points.shape
    voxels = voxel_slot.shape[0]
    serial_count, level_count = lax.axis_size("serial"), lax.axis_size("level")
    dma = pltpu.SemaphoreType.DMA
    slots = voxel_slot.reshape(1, voxels)
    counts = child_counts.reshape(1, voxels)
    ends = jnp.cumsum(counts, axis=1)
    starts = ends - counts
    tiles = jnp.arange(rows // TILE, dtype=jnp.int32) * TILE
    lows = jnp.minimum(jnp.sum((ends <= tiles[:, None]).astype(jnp.int32), axis=1) // 128, (voxels - SPAN) // 128)

    window, window_marks, slots_all, small, large = call(
        functools.partial(prologue_kernel, serial_count, level_count),
        [
            ((width, rows), BF16), ((1, rows), jnp.int32), ((serial_count, 1, voxels), jnp.int32),
            ((2, 4) + w_query0.shape[::-1], BF16), ((2, 6) + w_mlp_in.shape, BF16),
        ],
        vectors(points.T, patch_ids.reshape(1, rows), slots, w_query0.T, w_key0.T, w_value0.T, w_attn_out0,
                w_mlp_in, w_mlp_out.T, w_query1.T, w_key1.T, w_value1.T, w_attn_out1),
        [dma((3 + serial_count,)), dma((3 + serial_count,)), dma((2,))],
        collective=0,
    )
    shard = lax.axis_index("serial") * level_count + lax.axis_index("level")
    f = lax.axis_index("feat")
    place = jnp.arange(rows, dtype=jnp.int32)[None, :]
    before = (shard == 0) & (f == 0) & (place < PATCH)
    after = (shard == serial_count * level_count - 1) & (f == 1) & (place >= rows - PATCH)
    window_marks = jnp.where(before, -1, jnp.where(after, OUTSIDE, window_marks))
    half = rows // 2
    asked = window_marks[0, half // 2:half // 2 + half].reshape(-1, TILE)
    low = jnp.sum((window_marks < asked[:, :1]).astype(jnp.int32), axis=1) // TILE
    high = (jnp.sum((window_marks <= asked[:, -1:]).astype(jnp.int32), axis=1) + TILE - 1) // TILE
    ranges = jnp.stack([low, high], axis=1).reshape(-1)

    (fine_half,) = call(
        fine_kernel,
        [((width, half), BF16)],
        [("scalar", ranges)] + vectors(window, window_marks, small, large),
        [
            pltpu.VMEM((rows, width + HI_ROWS + LO_ROWS), BF16), pltpu.VMEM((width, rows), BF16),
            pltpu.VMEM((width, half), BF16), pltpu.VMEM((2 * PATCH + TILE, width // HEAD * TILE), F32),
        ],
    )
    (fine,) = call(swap_kernel, [((2, width, half), BF16)], vectors(fine_half), [dma((1,)), dma((1,))], collective=1)
    part = voxels // 2
    (pooled_part,) = call(
        pool_kernel,
        [((width, part), BF16)],
        [("scalar", lows)] + vectors(fine, starts, ends),
        [pltpu.VMEM((width, voxels), F32)],
    )

    wide = w_pool.shape[1]
    blocks = part // TILE
    each = 2 * serial_count - 1
    (nearby,) = call(
        functools.partial(coarse_kernel, serial_count, level_count),
        [((width, voxels), BF16)],
        vectors(pooled_part, slots_all, slots, large, w_pool, w_up.T),
        [
            pltpu.VMEM((serial_count, 2, width, part), BF16), pltpu.VMEM((serial_count, 2, blocks, width, TILE), BF16),
            pltpu.VMEM((width, part), F32), pltpu.VMEM((wide, part), BF16),
            pltpu.VMEM((part, wide), BF16), pltpu.VMEM((part, wide), BF16), pltpu.VMEM((width, voxels), F32),
            dma((each,)), dma((each,)), dma((blocks * each,)), dma((blocks * each,)),
        ],
        collective=2,
    )
    (refined,) = call(
        spread_kernel,
        [((width, rows), BF16)],
        [("scalar", lows)] + vectors(nearby, fine, starts, ends),
    )
    return refined.T


def solution(mesh):
    shards = ("groups", "serial", "level")
    columns, stacked = P(None, "feat"), P("feat", None)
    in_specs = (
        P(shards, None), P(shards), P(shards, None), P(shards),
        columns, columns, columns, stacked, columns, stacked, P(),
        columns, columns, columns, stacked, P(),
    )
    return jax.shard_map(local, mesh=mesh, in_specs=in_specs, out_specs=P(shards, None), check_vma=False)
```
